256 devices in a mesh: row: 32 (over y, z_hi, core), col: 8 (over z_lo, x).
Axes of the slice: x: 4, y: 4, z: 8 (z_hi: 4, z_lo: 2; z = z_hi * 2 + z_lo), core: 2. Of those that a mesh axis runs over, the one named last changes fastest.
Arguments:
- tokens: bfloat16 [1024, 8192], P('row', 'col'), may hold values from -6 to 6
- w_gate: bfloat16 [28672, 8192], P('row', 'col'), may hold values from -0.0625 to 0.0625
- w_up: bfloat16 [28672, 8192], P('row', 'col'), may hold values from -0.0625 to 0.0625
- w_down: bfloat16 [28672, 8192], P('row', 'col'), may hold values from -0.03125 to 0.03125
- grad_out: bfloat16 [1024, 8192], P('row', 'col'), may hold values from -6 to 6
Outputs:
- grad_in: bfloat16 [1024, 8192], P('row', 'col')
- grad_gate: bfloat16 [28672, 8192], P('row', 'col')
- grad_up: bfloat16 [28672, 8192], P('row', 'col')
- grad_down: bfloat16 [28672, 8192], P('row', 'col')
The draws below stay inside these ranges and needn't reach their ends.
All inputs are finite; a program needn't handle non-finite values.
Results may differ from the reference program's by a relative error of at most 0.03.
Values may be sent and summed in bfloat16 or wider, within the bound.
A program may use at most 128 MiB of HBM per device.

```python
import jax
import jax.numpy as jnp
from jax import lax

D = 8192
FF = 28672
TOKENS = 1024
N_COL = 8


def block_levels(own_key, shape, split, smallest, largest):
    gain, own = 1.0, jax.random.fold_in(own_key, 6)
    for axis_at, blocks in split:
        draws = jnp.exp(jax.random.uniform(jax.random.fold_in(own, axis_at), (blocks,), jnp.float32, smallest / len(split), largest / len(split)))
        gain = gain * jnp.repeat(draws, shape[axis_at] // blocks).reshape([-1 if axis == axis_at else 1 for axis in range(len(shape))])
    return gain


def normal_values(rng, shape, deviation, reach, cuts=(), dtype=jnp.bfloat16):
    gain = block_levels(rng, shape, cuts, -0.22, 0.18) if cuts else 1.0
    drawn = jax.random.normal(rng, shape, jnp.float32) * deviation * gain
    return jnp.minimum(jnp.maximum(drawn, -reach), reach).astype(dtype)


def setup_inputs(seed: int = 0) -> dict:
    arg_keys = jax.random.split(jax.random.key(seed), 6)
    return {
        "tokens": normal_values(arg_keys[0], (TOKENS, D), 1.0, 6.0, ((0, 32), (1, 8))),
        "w_gate": normal_values(arg_keys[1], (FF, D), D ** -0.5, 0.0625, ((0, 32), (1, 8))),
        "w_up": normal_values(arg_keys[2], (FF, D), D ** -0.5, 0.0625, ((0, 32), (1, 8))),
        "w_down": normal_values(arg_keys[3], (FF, D), FF ** -0.5, 0.03125, ((0, 32), (1, 8))),
        "grad_out": normal_values(arg_keys[4], (TOKENS, D), 1.0, 6.0, ((0, 32), (1, 8))),
    }


def blocks_sum(operand, weight):
    width = D // N_COL
    running = jnp.zeros((operand.shape[0], weight.shape[0]), jnp.float32)
    for block in range(N_COL):
        partial_sum = jnp.dot(operand[:, block * width:(block + 1) * width], weight[:, block * width:(block + 1) * width].T, preferred_element_type=jnp.float32)
        running = running + lax.optimization_barrier(partial_sum.astype(jnp.bfloat16)).astype(jnp.float32)
    return running


def reference(tokens, w_gate, w_up, w_down, grad_out):
    gate_pre = blocks_sum(tokens, w_gate)
    up_pre = blocks_sum(tokens, w_up)
    hid_grad = blocks_sum(grad_out, w_down)
    logistic = 1.0 / (1.0 + jnp.exp(-gate_pre))
    activated = gate_pre * logistic
    hidden = (activated * up_pre).astype(jnp.bfloat16)
    up_grad = (hid_grad * activated).astype(jnp.bfloat16)
    gate_grad = (hid_grad * up_pre * logistic * (1.0 + gate_pre * (1.0 - logistic))).astype(jnp.bfloat16)
    grad_in = jnp.dot(gate_grad, w_gate, preferred_element_type=jnp.float32) + jnp.dot(up_grad, w_up, preferred_element_type=jnp.float32)
    loss_scale = float(TOKENS) ** -0.5
    grad_gate = jnp.dot(gate_grad.T, tokens, preferred_element_type=jnp.float32) * loss_scale
    grad_up = jnp.dot(up_grad.T, tokens, preferred_element_type=jnp.float32) * loss_scale
    grad_down = jnp.dot(hidden.T, grad_out, preferred_element_type=jnp.float32) * loss_scale
    return (grad_in.astype(jnp.bfloat16), grad_gate.astype(jnp.bfloat16), grad_up.astype(jnp.bfloat16), grad_down.astype(jnp.bfloat16))
```

```python
import jax
import jax.numpy as jnp
from jax import lax
from jax.experimental import pallas as pl
from jax.experimental.pallas import tpu as pltpu
from jax.sharding import PartitionSpec as P

NY, NZ, NX = 4, 4, 4
F32, BF16 = jnp.float32, jnp.bfloat16


def mm(a, b, dims):
    return lax.dot_general(a, b, (dims, ((), ())), preferred_element_type=F32)


def body(
    tok_hbm, wg_hbm, wu_hbm, wd_hbm, out_hbm,
    gin_hbm, dg_hbm, du_hbm, dd_hbm,
    tg, w, px, rxt, rxf, rz, pz, rzz, rzt, rzf, az, ax, acc, stage, trans,
    go, gs, gc, ys, yt, yf, zs, zr, gout,
    send, recv, local,
):
    row, col = lax.axis_index("row"), lax.axis_index("col")
    y, zh, core = row // 8, (row // 2) % 4, row % 2
    zl, x = col // 4, col % 4

    def at_row(y_, zh_, core_):
        return {"row": (y_ * 4 + zh_) * 2 + core_, "col": col}

    def at_col(zl_, x_):
        return {"row": row, "col": zl_ * 4 + x_}

    y_up, y_dn = at_row((y + 1) % 4, zh, core), at_row((y + 3) % 4, zh, core)
    zh_at = [None] + [at_row(y, (zh + d) % 4, core) for d in (1, 2, 3)]
    twin = at_row(y, zh, 1 - core)
    x_up, x_dn = at_col(zl, (x + 1) % 4), at_col(zl, (x + 3) % 4)
    z_pair = at_col(1 - zl, x)
    partners = [y_up, y_dn, zh_at[1], zh_at[2], zh_at[3], twin, x_up, x_dn, z_pair]

    counts = {"remote": 0, "local": 0}
    remote = {}

    def push(key, src, dst, device):
        n = counts["remote"]
        counts["remote"] = n + 1
        copy = pltpu.make_async_remote_copy(
            src_ref=src, dst_ref=dst, send_sem=send.at[n], recv_sem=recv.at[n],
            device_id=device, device_id_type=pl.DeviceIdType.MESH,
        )
        copy.start()
        assert key not in remote
        remote[key] = copy

    def arrive(*keys):
        for key in keys:
            remote[key].wait_recv()

    def move(src, dst):
        n = counts["local"]
        counts["local"] = n + 1
        copy = pltpu.make_async_copy(src, dst, local.at[n])
        copy.start()
        return copy

    d_model = w.shape[-1]
    ffb = w.shape[-2]
    cut = -(-ffb // 32) * 16
    chunk = px.shape[-1]
    halves = (pl.ds(0, cut), pl.ds(cut, ffb - cut))
    n_tile = min(256, d_model)

    def hbm_rows(j, h):
        first = ((x + j) % 4) * (2 * ffb) + (zl if h == 0 else 1 - zl) * ffb
        return pl.ds(pl.multiple_of(first, 16), ffb)

    tok_in = [move(tok_hbm, tg.at[0, 0, 0, 0]), move(out_hbm, tg.at[1, 0, 0, 0])]
    w_in = [
        [move(src.at[hbm_rows(j, h)], w.at[k, j, h]) for j in range(4) for h in range(2)]
        for k, src in enumerate((wg_hbm, wu_hbm, wd_hbm))
    ]

    barrier = pltpu.get_barrier_semaphore()
    for partner in partners:
        pl.semaphore_signal(barrier, inc=1, device_id=partner, device_id_type=pl.DeviceIdType.MESH)
    for copy in tok_in:
        copy.wait()
    pl.semaphore_wait(barrier, len(partners))

    def gather_start(s):
        own = tg.at[s, 0, 0, 0]
        for d in (2, 1, 3):
            push(("az", s, d), own, tg.at[s, 0, 0, 4 - d], zh_at[d])
        push(("ac", s, 0), own, tg.at[s, 0, 1, 0], twin)

    def gather_z(s):
        arrive(("az", s, 1), ("az", s, 2), ("az", s, 3))
        push(("ay", s, 1), tg.at[s, 0, 0], tg.at[s, 3, 0], y_up)
        push(("ay", s, 3), tg.at[s, 0, 0], tg.at[s, 1, 0], y_dn)
        push(("ac", s, 1), tg.at[s, 0, 0, pl.ds(1, 3)], tg.at[s, 0, 1, pl.ds(1, 3)], twin)

    def gather_y(s):
        arrive(("ay", s, 1), ("ay", s, 3))
        push(("at", s, 1), tg.at[s, 3, 0, pl.ds(0, 2)], tg.at[s, 2, 0, pl.ds(0, 2)], y_up)
        push(("at", s, 3), tg.at[s, 1, 0, pl.ds(2, 2)], tg.at[s, 2, 0, pl.ds(2, 2)], y_dn)
        push(("af", s, 1), tg.at[s, 1, 0], tg.at[s, 1, 1], twin)
        push(("af", s, 3), tg.at[s, 3, 0], tg.at[s, 3, 1], twin)

    def gather_t(s):
        arrive(("at", s, 1), ("at", s, 3))
        push(("af", s, 2), tg.at[s, 2, 0], tg.at[s, 2, 1], twin)

    def gathered(s, i):
        if i == 0:
            arrive(("ac", s, 0), ("ac", s, 1))
        else:
            arrive(("af", s, i))

    def rows_of(s, i):
        return tg[s, i].reshape(chunk, d_model)

    def product(k, s, i, pair):
        part = w[k, 2 * pair:2 * pair + 2].reshape(4 * ffb, d_model)
        out = mm(part, rows_of(s, i), ((1,), (1,)))
        return out.astype(BF16).reshape(2, 2, ffb, chunk)

    def gate_up_start(i):
        if i == 0:
            for copy in w_in[0] + w_in[1]:
                copy.wait()
        gathered(0, i)
        for pair in (1, 0):
            for k in (0, 1):
                px[i, 2 * pair:2 * pair + 2, :, k] = product(k, 0, i, pair)
            if pair == 1:
                push(("xt", i, 0), px.at[i, 2, 0], rxt.at[i, 0], x_up)
                push(("xt", i, 1), px.at[i, 2, 1], rxt.at[i, 1], x_dn)
                push(("xf", i, 1, 0), px.at[i, 3, 0], rxf.at[i, 1, 0], x_dn)
            else:
                push(("xf", i, 0, 1), px.at[i, 1, 1], rxf.at[i, 0, 1], x_up)

    def gate_up_pass(i):
        arrive(("xt", i, 0))
        px[i, 1, 0] = (px[i, 1, 0].astype(F32) + rxt[i, 0].astype(F32)).astype(BF16)
        push(("xf", i, 0, 0), px.at[i, 1, 0], rxf.at[i, 0, 0], x_up)
        arrive(("xt", i, 1))
        px[i, 3, 1] = (px[i, 3, 1].astype(F32) + rxt[i, 1].astype(F32)).astype(BF16)
        push(("xf", i, 1, 1), px.at[i, 3, 1], rxf.at[i, 1, 1], x_dn)

    def gate_up_sum(i, h):
        return px[i, 0, h].astype(F32) + rxf[i, 0, h].astype(F32) + rxf[i, 1, h].astype(F32)

    def gate_up_cross(i):
        arrive(("xf", i, 0, 0), ("xf", i, 0, 1), ("xf", i, 1, 0), ("xf", i, 1, 1))
        px[i, 0, 1] = gate_up_sum(i, 1).astype(BF16)
        push(("xz", i), px.at[i, 0, 1], rz.at[i], z_pair)

    def hid_start(i):
        if i == 0:
            for copy in w_in[2]:
                copy.wait()
        gathered(1, i)
        for pair in (1, 0):
            out = product(2, 1, i, pair)
            for j in range(2):
                for h in range(2):
                    pz[i, h, 2 * pair + j] = out[j, h]
        push(("zz", i), pz.at[i, 1], rzz.at[i], z_pair)

    def hid_cross(i):
        arrive(("zz", i))
        pz[i, 0] = (pz[i, 0].astype(F32) + rzz[i].astype(F32)).astype(BF16)
        for ab, (to, back, far, near) in enumerate(((x_up, x_dn, 0, 3), (x_dn, x_up, 1, 1))):
            push(("zt", i, ab), pz.at[i, 0, 2, halves[ab]], rzt.at[i, halves[ab]], to)
        push(("zf", i, 1, 0), pz.at[i, 0, 3, halves[0]], rzf.at[i, 1, halves[0]], x_dn)
        push(("zf", i, 0, 1), pz.at[i, 0, 1, halves[1]], rzf.at[i, 0, halves[1]], x_up)

    def hid_pass(i):
        for ab, (j, to) in enumerate(((1, x_up), (3, x_dn))):
            arrive(("zt", i, ab))
            part = pz[i, 0, j, halves[ab]].astype(F32) + rzt[i, halves[ab]].astype(F32)
            pz[i, 0, j, halves[ab]] = part.astype(BF16)
            push(("zf", i, ab, ab), pz.at[i, 0, j, halves[ab]], rzf.at[i, ab, halves[ab]], to)

    def pointwise(i):
        arrive(("xz", i))
        pre = gate_up_sum(i, 0) + rz[i].astype(F32)
        gate_pre, up_pre = pre[0], pre[1]
        arrive(("zf", i, 0, 0), ("zf", i, 0, 1), ("zf", i, 1, 0), ("zf", i, 1, 1))
        hid_grad = pz[i, 0, 0].astype(F32) + rzf[i, 0].astype(F32) + rzf[i, 1].astype(F32)
        logistic = 1.0 / (1.0 + jnp.exp(-gate_pre))
        activated = gate_pre * logistic
        az[i, 0, 0, 0] = (hid_grad * up_pre * logistic * (1.0 + gate_pre * (1.0 - logistic))).astype(BF16)
        az[i, 0, 0, 1] = (hid_grad * activated).astype(BF16)
        push(("gz", i), az.at[i, 0, 0], az.at[i, 0, 1], z_pair)
        push(("gx", i, 0, 0), az.at[i, 0, 0], az.at[i, 3, 0], x_up)
        push(("gx", i, 1, 0), az.at[i, 0, 0], az.at[i, 1, 0], x_dn)
        ax[i, 0, 0] = (activated * up_pre).astype(BF16)
        push(("hx", i, 0), ax.at[i, 0, 0], ax.at[i, 0, 3], x_up)
        push(("hx", i, 1), ax.at[i, 0, 0], ax.at[i, 0, 1], x_dn)
        push(("hz", i, 0), ax.at[i, 0, 0], ax.at[i, 1, 0], z_pair)

    def spread_pair(i):
        arrive(("gz", i))
        push(("gx", i, 0, 1), az.at[i, 0, 1], az.at[i, 3, 1], x_up)
        push(("gx", i, 1, 1), az.at[i, 0, 1], az.at[i, 1, 1], x_dn)

    def spread_far(i):
        arrive(("hx", i, 0), ("hx", i, 1))
        push(("ht", i, 0), ax.at[i, 0, 3, halves[0]], ax.at[i, 0, 2, halves[0]], x_up)
        push(("ht", i, 1), ax.at[i, 0, 1, halves[1]], ax.at[i, 0, 2, halves[1]], x_dn)
        arrive(("gx", i, 0, 0))
        push(("gt", i, 0), az.at[i, 3, 0], az.at[i, 2, 0], x_up)
        push(("hz", i, 1), ax.at[i, 0, 1], ax.at[i, 1, 1], z_pair)
        push(("hz", i, 3), ax.at[i, 0, 3], ax.at[i, 1, 3], z_pair)
        arrive(("gx", i, 1, 1))
        push(("gt", i, 1), az.at[i, 1, 1], az.at[i, 2, 1], x_dn)

    def spread_last(i):
        arrive(("ht", i, 0), ("ht", i, 1))
        push(("hz", i, 2), ax.at[i, 0, 2], ax.at[i, 1, 2], z_pair)

    def input_rows(i):
        arrive(("gx", i, 1, 0), ("gx", i, 0, 1), ("gt", i, 0), ("gt", i, 1))
        for k in (0, 1):
            trans[k] = az[i, :, :, k].reshape(8 * ffb, chunk).T
        for n in range(d_model // n_tile):
            cols = pl.ds(n * n_tile, n_tile)
            out = sum(
                mm(trans[k], w[k, :, :, :, cols].reshape(8 * ffb, n_tile), ((1,), (0,)))
                for k in (0, 1)
            )
            go[i, :, cols] = out[:chunk // 2]
            gs[i, :, cols] = out[chunk // 2:].astype(BF16)
        push(("cc", i), gs.at[i], gc.at[i], twin)

    n_half = chunk // 4
    top, low = pl.ds(0, n_half), pl.ds(n_half, n_half)

    def input_fold(i):
        arrive(("cc", i))
        if i == 0:
            go[0] = go[0] + gc[0].astype(F32)
        elif i == 1:
            ys[1] = (go[1] + gc[1].astype(F32)).astype(BF16)
            push(("yf", 0, 1), ys.at[1, low], yf.at[0, low], y_up)
        elif i == 2:
            ys[2] = (go[2] + gc[2].astype(F32)).astype(BF16)
            push(("yt", 0), ys.at[2, top], yt.at[0], y_up)
            push(("yt", 1), ys.at[2, low], yt.at[1], y_dn)
        else:
            ys[3, top] = (go[3, top] + gc[3, top].astype(F32)).astype(BF16)
            push(("yf", 1, 0), ys.at[3, top], yf.at[1, top], y_dn)
            arrive(("yt", 1))
            ys[3, low] = (go[3, low] + gc[3, low].astype(F32) + yt[1].astype(F32)).astype(BF16)
            push(("yf", 1, 1), ys.at[3, low], yf.at[1, low], y_dn)
            arrive(("yt", 0))
            ys[1, top] = (ys[1, top].astype(F32) + yt[0].astype(F32)).astype(BF16)
            push(("yf", 0, 0), ys.at[1, top], yf.at[0, top], y_up)

    def input_own():
        arrive(("yf", 0, 0), ("yf", 0, 1), ("yf", 1, 0), ("yf", 1, 1))
        go[0] = go[0] + yf[0].astype(F32) + yf[1].astype(F32)
        piece = chunk // 8
        for d in (2, 1, 3):
            zs[d] = go[0, d * piece:(d + 1) * piece].astype(BF16)
            push(("zr", d), zs.at[d], zr.at[d], zh_at[d])

    def input_out():
        piece = chunk // 8
        arrive(("zr", 1), ("zr", 2), ("zr", 3))
        gout[...] = (
            go[0, :piece] + zr[1].astype(F32) + zr[2].astype(F32) + zr[3].astype(F32)
        ).astype(BF16)
        return move(gout, gin_hbm)

    scale = float(NY * chunk) ** -0.5
    writes = []

    def weight_rows(k, i):
        left = az[i, :, :, k] if k < 2 else None
        s = 0 if k < 2 else 1
        for pair in (0, 1):
            js = slice(2 * pair, 2 * pair + 2)
            if k < 2:
                left = az[i, js, :, k].reshape(4 * ffb, chunk)
            else:
                left = jnp.concatenate(
                    [ax[i, h, j] for j in (2 * pair, 2 * pair + 1) for h in (0, 1)], axis=0
                )
            for n in range(d_model // n_tile):
                cols = pl.ds(n * n_tile, n_tile)
                right = tg[s, i, :, :, :, cols].reshape(chunk, n_tile)
                out = mm(left, right, ((1,), (0,))).reshape(2, 2, ffb, n_tile)
                if i > 0:
                    out = out + acc[k, js, :, :, cols]
                if i < NY - 1:
                    acc[k, js, :, :, cols] = out
                else:
                    stage[k, js, :, :, cols] = (out * scale).astype(BF16)
            if i == NY - 1:
                out_hbm_k = (dg_hbm, du_hbm, dd_hbm)[k]
                for j in (2 * pair, 2 * pair + 1):
                    for h in range(2):
                        writes.append(move(stage.at[k, j, h], out_hbm_k.at[hbm_rows(j, h)]))

    def weight_gate_up(i):
        weight_rows(0, i)
        weight_rows(1, i)

    def weight_down(i):
        arrive(("hz", i, 0), ("hz", i, 1), ("hz", i, 2), ("hz", i, 3))
        weight_rows(2, i)

    gather_start(0)
    gather_start(1)
    gather_z(0)
    gate_up_start(0)
    gather_z(1)
    hid_start(0)
    gather_y(0)
    gate_up_pass(0)
    hid_cross(0)
    gather_y(1)
    gate_up_start(1)
    gate_up_cross(0)
    hid_start(1)
    hid_pass(0)
    gather_t(0)
    gather_t(1)
    gate_up_pass(1)
    hid_cross(1)
    pointwise(0)
    gate_up_start(2)
    gate_up_cross(1)
    spread_pair(0)
    hid_start(2)
    hid_pass(1)
    spread_far(0)
    gate_up_pass(2)
    hid_cross(2)
    pointwise(1)
    spread_last(0)
    gate_up_start(3)
    gate_up_cross(2)
    spread_pair(1)
    hid_start(3)
    hid_pass(2)
    input_rows(0)
    spread_far(1)
    gate_up_pass(3)
    hid_cross(3)
    pointwise(2)
    spread_last(1)
    input_fold(0)
    weight_gate_up(0)
    gate_up_cross(3)
    spread_pair(2)
    hid_pass(3)
    input_rows(1)
    spread_far(2)
    pointwise(3)
    spread_last(2)
    input_fold(1)
    weight_down(0)
    spread_pair(3)
    weight_gate_up(1)
    input_rows(2)
    spread_far(3)
    input_fold(2)
    weight_down(1)
    spread_last(3)
    weight_gate_up(2)
    input_rows(3)
    weight_down(2)
    input_fold(3)
    weight_gate_up(3)
    input_own()
    weight_down(3)
    writes.append(input_out())
    for copy in remote.values():
        copy.wait_send()
    for copy in writes:
        copy.wait()


def local(tokens, w_gate, w_up, w_down, grad_out):
    piece, d = tokens.shape
    ff = w_gate.shape[0]
    ffb, chunk = ff // 8, 8 * piece
    hbm = pl.BlockSpec(memory_space=pl.ANY)

    def vmem(*shape, dtype=BF16):
        return pltpu.VMEM(shape, dtype)

    scratch = [
        vmem(2, 4, 2, 4, piece, d),
        vmem(3, 4, 2, ffb, d),
        vmem(4, 4, 2, 2, ffb, chunk),
        vmem(4, 2, 2, ffb, chunk),
        vmem(4, 2, 2, 2, ffb, chunk),
        vmem(4, 2, ffb, chunk),
        vmem(4, 2, 4, ffb, chunk),
        vmem(4, 4, ffb, chunk),
        vmem(4, ffb, chunk),
        vmem(4, 2, ffb, chunk),
        vmem(4, 4, 2, 2, ffb, chunk),
        vmem(4, 2, 4, ffb, chunk),
        vmem(3, 4, 2, ffb, d, dtype=F32),
        vmem(3, 4, 2, ffb, d),
        vmem(2, chunk, 8 * ffb),
        vmem(4, chunk // 2, d, dtype=F32),
        vmem(4, chunk // 2, d),
        vmem(4, chunk // 2, d),
        vmem(4, chunk // 2, d),
        vmem(2, chunk // 4, d),
        vmem(2, chunk // 2, d),
        vmem(4, piece, d),
        vmem(4, piece, d),
        vmem(piece, d),
        pltpu.SemaphoreType.DMA((160,)),
        pltpu.SemaphoreType.DMA((160,)),
        pltpu.SemaphoreType.DMA((56,)),
    ]
    weight = jax.ShapeDtypeStruct((ff, d), BF16)
    return pl.pallas_call(
        body,
        out_shape=(jax.ShapeDtypeStruct((piece, d), BF16), weight, weight, weight),
        in_specs=[hbm] * 5,
        out_specs=(hbm,) * 4,
        scratch_shapes=scratch,
        compiler_params=pltpu.CompilerParams(
            collective_id=0, has_side_effects=True, vmem_limit_bytes=60 * 2 ** 20
        ),
        cost_estimate=pl.CostEstimate(
            flops=16 * 4 * chunk * ff * d, bytes_accessed=12 * ff * d, transcendentals=4 * chunk * ffb
        ),
    )(tokens, w_gate, w_up, w_down, grad_out)


def solution(mesh):
    spec = P("row", "col")
    return jax.shard_map(
        local, mesh=mesh, in_specs=(spec,) * 5, out_specs=(spec,) * 4, check_vma=False
    )
```

```python
import jax
import jax.numpy as jnp
from jax import lax
from jax.experimental import pallas as pl
from jax.experimental.pallas import tpu as pltpu
from jax.sharding import PartitionSpec as P

NY, NZ, NX = 4, 4, 4
F32, BF16 = jnp.float32, jnp.bfloat16
HAND_PARTS = 4


def mm(a, b, dims):
    return lax.dot_general(a, b, (dims, ((), ())), preferred_element_type=F32)


def body(
    tok_hbm, wg_hbm, wu_hbm, wd_hbm, out_hbm,
    gin_hbm, dg_hbm, du_hbm, dd_hbm,
    tg, w, px, rxt, rxf, rz, pz, rzz, rzt, rzf, az, ax, acc, stage, trans,
    part, gs, gc, ys, yt, yf, zs, zq, zr, gout,
    send, recv, local,
):
    row, col = lax.axis_index("row"), lax.axis_index("col")
    y, zh, core = row // 8, (row // 2) % 4, row % 2
    zl, x = col // 4, col % 4

    def at_row(y_, zh_, core_):
        return {"row": (y_ * 4 + zh_) * 2 + core_, "col": col}

    def at_col(zl_, x_):
        return {"row": row, "col": zl_ * 4 + x_}

    y_up, y_dn = at_row((y + 1) % 4, zh, core), at_row((y + 3) % 4, zh, core)
    zh_up, zh_dn = at_row(y, (zh + 1) % 4, core), at_row(y, (zh + 3) % 4, core)
    twin = at_row(y, zh, 1 - core)
    x_up, x_dn = at_col(zl, (x + 1) % 4), at_col(zl, (x + 3) % 4)
    z_pair = at_col(1 - zl, x)
    partners = [y_up, y_dn, zh_up, zh_dn, twin, x_up, x_dn, z_pair]

    sends, groups, arrived = {}, {}, set()
    sent_refs = {
        "xt": rxt, "xf": rxf, "xz": rz, "zz": rzz, "zt": rzt, "zf": rzf,
        "gz": az.at[:, 0, 1], "gx0": az.at[:, 3], "gx1": az.at[:, 1], "gt": az.at[:, 2],
        "hx0": ax.at[:, 0, 3], "hx1": ax.at[:, 0, 1], "ht": ax.at[:, 0, 2], "hz": ax.at[:, 1],
        "cc": gc, "yt": yt, "yf": yf, "zq": zq, "zr": zr,
        "az1": tg.at[3, 0, 0], "az3": tg.at[1, 0, 0], "at": tg.at[2, 0, 0],
        "ay1": tg.at[:, 0, 3], "ay3": tg.at[:, 0, 1], "ax": tg.at[:, 0, 2], "ac": tg.at[:, 1],
    }

    def copy_of(src, dst, send_at, recv_at, device):
        return pltpu.make_async_remote_copy(
            src_ref=src, dst_ref=dst, send_sem=send.at[send_at], recv_sem=recv.at[recv_at],
            device_id=device, device_id_type=pl.DeviceIdType.MESH,
        )

    def push(key, src, dst, device, whole=None):
        send_at = sends.setdefault(key[0], len(sends))
        recv_at, _ = groups.setdefault(key, (len(groups), dst if whole is None else whole))
        copy_of(src, dst, send_at, recv_at, device).start()

    def arrive(*keys):
        for key in keys:
            if key not in arrived:
                arrived.add(key)
                recv_at, whole = groups[key]
                copy_of(whole, whole, 0, recv_at, twin).wait_recv()

    def all_sent():
        for kind, send_at in sends.items():
            copy_of(sent_refs[kind], sent_refs[kind], send_at, 0, twin).wait_send()

    def move(n, src, dst):
        copy = pltpu.make_async_copy(src, dst, local.at[n])
        copy.start()
        return copy

    def moved(n, whole):
        pltpu.make_async_copy(whole, whole, local.at[n]).wait()

    d_model = w.shape[-1]
    ffb = w.shape[-2]
    cut = -(-ffb // 32) * 16
    chunk = px.shape[-1]
    halves = (pl.ds(0, cut), pl.ds(cut, ffb - cut))
    n_tile = min(256, d_model)

    def hbm_rows(j, h):
        first = ((x + j) % 4) * (2 * ffb) + (zl if h == 0 else 1 - zl) * ffb
        return pl.ds(pl.multiple_of(first, 16), ffb)

    tok_in = [move(6, tok_hbm, tg.at[0, 0, 0, 0]), move(7, out_hbm, tg.at[0, 0, 0, 1])]
    for k, src in enumerate((wg_hbm, wu_hbm, wd_hbm)):
        for j in range(4):
            for h in range(2):
                move(k, src.at[hbm_rows(j, h)], w.at[k, j, h])

    barrier = pltpu.get_barrier_semaphore()
    for partner in partners:
        pl.semaphore_signal(barrier, inc=1, device_id=partner, device_id_type=pl.DeviceIdType.MESH)
    for copy in tok_in:
        copy.wait()
    pl.semaphore_wait(barrier, len(partners))

    half = chunk // 16
    first, second = pl.ds(0, half), pl.ds(half, half)
    both = pl.ds(0, 2)

    def gather_start():
        for s in (0, 1):
            own = tg.at[0, 0, 0, s]
            push(("ay1", 0, s), own, tg.at[0, 0, 3, s], y_up)
            push(("ay3", 0, s), own, tg.at[0, 0, 1, s], y_dn)
            push(("ac", 0, s), own, tg.at[0, 1, 0, s], twin, tg.at[0, 1, :, s])
            push(("az1", s), own, tg.at[3, 0, 0, s], zh_up)
            push(("az3", s), own, tg.at[1, 0, 0, s], zh_dn)

    def gather_z():
        arrive(("az1", 0), ("az1", 1))
        push(("at",), tg.at[3, 0, 0, :, first], tg.at[2, 0, 0, :, first], zh_up, tg.at[2, 0, 0])
        arrive(("az3", 0), ("az3", 1))
        push(("at",), tg.at[1, 0, 0, :, second], tg.at[2, 0, 0, :, second], zh_dn, tg.at[2, 0, 0])

    def kind(c, s):
        return s if c < 2 else both

    def gather_y(c, s):
        if c == 1:
            arrive(("az3", s))
        elif c == 3:
            arrive(("az1", 0), ("az1", 1))
        else:
            arrive(("at",))
        own = tg.at[c, 0, 0, kind(c, s)]
        push(("ay1", c, s), own, tg.at[c, 0, 3, kind(c, s)], y_up)
        push(("ay3", c, s), own, tg.at[c, 0, 1, kind(c, s)], y_dn)

    def gather_far(c, s):
        far = tg.at[c, 0, 2, kind(c, s)]
        arrive(("ay1", c, s))
        push(("ax", c, s), tg.at[c, 0, 3, kind(c, s), first], tg.at[c, 0, 2, kind(c, s), first], y_up, far)
        arrive(("ay3", c, s))
        push(("ax", c, s), tg.at[c, 0, 1, kind(c, s), second], tg.at[c, 0, 2, kind(c, s), second], y_dn, far)
        if c == 0:
            for yr in (1, 3):
                push(("ac", c, s), tg.at[c, 0, yr, s], tg.at[c, 1, yr, s], twin, tg.at[0, 1, :, s])

    def gather_twin(c, s):
        arrive(("ax", c, s))
        if c == 0:
            push(("ac", c, s), tg.at[c, 0, 2, s], tg.at[c, 1, 2, s], twin, tg.at[0, 1, :, s])
        else:
            push(("ac", c, s), tg.at[c, 0, :, kind(c, s)], tg.at[c, 1, :, kind(c, s)], twin)

    def gathered(s, c):
        arrive(("ac", c, s if c < 2 else 0))

    def rows_of(s, c):
        return tg[c, :, :, s].reshape(chunk, d_model)

    def product(k, s, i, pair):
        part = w[k, 2 * pair:2 * pair + 2].reshape(4 * ffb, d_model)
        out = mm(part, rows_of(s, i), ((1,), (1,)))
        return out.astype(BF16).reshape(2, 2, ffb, chunk)

    def gate_up_start(i):
        if i == 0:
            moved(0, w.at[0])
            moved(1, w.at[1])
        gathered(0, i)
        for pair in (1, 0):
            for k in (0, 1):
                px[i, 2 * pair:2 * pair + 2, :, k] = product(k, 0, i, pair)
            if pair == 1:
                push(("xt", i), px.at[i, 2, 0], rxt.at[i, 0], x_up, rxt.at[i])
                push(("xt", i), px.at[i, 2, 1], rxt.at[i, 1], x_dn, rxt.at[i])
                push(("xf", i), px.at[i, 3, 0], rxf.at[i, 1, 0], x_dn, rxf.at[i])
            else:
                push(("xf", i), px.at[i, 1, 1], rxf.at[i, 0, 1], x_up, rxf.at[i])

    def gate_up_pass(i):
        arrive(("xt", i))
        px[i, 1, 0] = (px[i, 1, 0].astype(F32) + rxt[i, 0].astype(F32)).astype(BF16)
        push(("xf", i), px.at[i, 1, 0], rxf.at[i, 0, 0], x_up, rxf.at[i])
        px[i, 3, 1] = (px[i, 3, 1].astype(F32) + rxt[i, 1].astype(F32)).astype(BF16)
        push(("xf", i), px.at[i, 3, 1], rxf.at[i, 1, 1], x_dn, rxf.at[i])

    def gate_up_sum(i, h):
        return px[i, 0, h].astype(F32) + rxf[i, 0, h].astype(F32) + rxf[i, 1, h].astype(F32)

    def gate_up_cross(i):
        arrive(("xf", i))
        px[i, 0, 1] = gate_up_sum(i, 1).astype(BF16)
        push(("xz", i), px.at[i, 0, 1], rz.at[i], z_pair)

    def hid_start(i):
        if i == 0:
            moved(2, w.at[2])
        gathered(1, i)
        for pair in (1, 0):
            out = product(2, 1, i, pair)
            for j in range(2):
                for h in range(2):
                    pz[i, h, 2 * pair + j] = out[j, h]
        push(("zz", i), pz.at[i, 1], rzz.at[i], z_pair)

    def hid_cross(i):
        arrive(("zz", i))
        pz[i, 0] = (pz[i, 0].astype(F32) + rzz[i].astype(F32)).astype(BF16)
        for ab, (to, back, far, near) in enumerate(((x_up, x_dn, 0, 3), (x_dn, x_up, 1, 1))):
            push(("zt", i), pz.at[i, 0, 2, halves[ab]], rzt.at[i, halves[ab]], to, rzt.at[i])
        push(("zf", i), pz.at[i, 0, 3, halves[0]], rzf.at[i, 1, halves[0]], x_dn, rzf.at[i])
        push(("zf", i), pz.at[i, 0, 1, halves[1]], rzf.at[i, 0, halves[1]], x_up, rzf.at[i])

    def hid_pass(i):
        arrive(("zt", i))
        for ab, (j, to) in enumerate(((1, x_up), (3, x_dn))):
            part = pz[i, 0, j, halves[ab]].astype(F32) + rzt[i, halves[ab]].astype(F32)
            pz[i, 0, j, halves[ab]] = part.astype(BF16)
            push(("zf", i), pz.at[i, 0, j, halves[ab]], rzf.at[i, ab, halves[ab]], to, rzf.at[i])

    def pointwise(i):
        arrive(("xz", i))
        pre = gate_up_sum(i, 0) + rz[i].astype(F32)
        gate_pre, up_pre = pre[0], pre[1]
        arrive(("zf", i))
        hid_grad = pz[i, 0, 0].astype(F32) + rzf[i, 0].astype(F32) + rzf[i, 1].astype(F32)
        logistic = 1.0 / (1.0 + jnp.exp(-gate_pre))
        activated = gate_pre * logistic
        az[i, 0, 0, 0] = (hid_grad * up_pre * logistic * (1.0 + gate_pre * (1.0 - logistic))).astype(BF16)
        az[i, 0, 0, 1] = (hid_grad * activated).astype(BF16)
        push(("gz", i), az.at[i, 0, 0], az.at[i, 0, 1], z_pair)
        push(("gx0", i, 0), az.at[i, 0, 0], az.at[i, 3, 0], x_up)
        push(("gx1", i, 0), az.at[i, 0, 0], az.at[i, 1, 0], x_dn)
        ax[i, 0, 0] = (activated * up_pre).astype(BF16)

    def spread_pair(i):
        arrive(("gz", i))
        push(("gx0", i, 1), az.at[i, 0, 1], az.at[i, 3, 1], x_up)
        push(("gx1", i, 1), az.at[i, 0, 1], az.at[i, 1, 1], x_dn)

    def spread_far(i):
        arrive(("gx0", i, 0))
        push(("gt", i), az.at[i, 3, 0], az.at[i, 2, 0], x_up, az.at[i, 2])
        arrive(("gx1", i, 1))
        push(("gt", i), az.at[i, 1, 1], az.at[i, 2, 1], x_dn, az.at[i, 2])

    def down_start(i):
        push(("hx0", i), ax.at[i, 0, 0], ax.at[i, 0, 3], x_up)
        push(("hx1", i), ax.at[i, 0, 0], ax.at[i, 0, 1], x_dn)
        push(("hz", i), ax.at[i, 0, 0], ax.at[i, 1, 0], z_pair, ax.at[i, 1])

    def down_far(i):
        arrive(("hx0", i))
        push(("ht", i), ax.at[i, 0, 3, halves[0]], ax.at[i, 0, 2, halves[0]], x_up, ax.at[i, 0, 2])
        push(("hz", i), ax.at[i, 0, 3], ax.at[i, 1, 3], z_pair, ax.at[i, 1])
        arrive(("hx1", i))
        push(("ht", i), ax.at[i, 0, 1, halves[1]], ax.at[i, 0, 2, halves[1]], x_dn, ax.at[i, 0, 2])
        push(("hz", i), ax.at[i, 0, 1], ax.at[i, 1, 1], z_pair, ax.at[i, 1])

    def down_last(i):
        arrive(("ht", i))
        push(("hz", i), ax.at[i, 0, 2], ax.at[i, 1, 2], z_pair, ax.at[i, 1])

    def input_near(i):
        arrive(("gz", i), ("gx0", i, 0), ("gx1", i, 1), ("gx1", i, 0), ("gx0", i, 1))
        for j in (0, 1, 3):
            for k in (0, 1):
                trans[k, j] = az[i, j, :, k].reshape(2 * ffb, chunk).T
        for n in range(d_model // n_tile):
            cols = pl.ds(n * n_tile, n_tile)
            part[i, :, cols] = sum(
                mm(trans[k, j], w[k, j, :, :, cols].reshape(2 * ffb, n_tile), ((1,), (0,)))
                for k in (0, 1) for j in (0, 1, 3)
            )

    def input_rows(i):
        arrive(("gt", i))
        for k in (0, 1):
            trans[k, 2] = az[i, 2, :, k].reshape(2 * ffb, chunk).T
        for n in range(d_model // n_tile):
            cols = pl.ds(n * n_tile, n_tile)
            out = part[i, :, cols] + sum(
                mm(trans[k, 2], w[k, 2, :, :, cols].reshape(2 * ffb, n_tile), ((1,), (0,)))
                for k in (0, 1)
            )
            part[i, :chunk // 2, cols] = out[:chunk // 2]
            gs[i, :, cols] = out[chunk // 2:].astype(BF16)
        push(("cc", i), gs.at[i], gc.at[i], twin)

    piece = chunk // 8

    def at_y(yr):
        return pl.ds(yr * piece, piece)

    def input_fold(i):
        arrive(("cc", i))
        part[i, at_y(0)] = part[i, at_y(0)] + gc[i, at_y(0)].astype(F32)
        for yr in (2, 1, 3):
            ys[i, yr] = (part[i, at_y(yr)] + gc[i, at_y(yr)].astype(F32)).astype(BF16)
            if yr == 2:
                push(("yt", i), ys.at[i, 2, first], yt.at[i, first], y_up, yt.at[i])
                push(("yt", i), ys.at[i, 2, second], yt.at[i, second], y_dn, yt.at[i])
            elif yr == 1:
                push(("yf", i), ys.at[i, 1, second], yf.at[i, 0, second], y_up, yf.at[i])
            else:
                push(("yf", i), ys.at[i, 3, first], yf.at[i, 1, first], y_dn, yf.at[i])

    def input_pass(i):
        arrive(("yt", i))
        for ab, (yr, rows, to) in enumerate(((1, first, y_up), (3, second, y_dn))):
            ys[i, yr, rows] = (ys[i, yr, rows].astype(F32) + yt[i, rows].astype(F32)).astype(BF16)
            push(("yf", i), ys.at[i, yr, rows], yf.at[i, ab, rows], to, yf.at[i])

    def input_own(i):
        arrive(("yf", i))
        part[i, at_y(0)] = part[i, at_y(0)] + yf[i, 0].astype(F32) + yf[i, 1].astype(F32)
        if i == 1:
            zs[1, second] = part[1, pl.ds(half, half)].astype(BF16)
            push(("zr",), zs.at[1, second], zr.at[0, second], zh_up, zr)
        elif i == 2:
            zs[2] = part[2, at_y(0)].astype(BF16)
            push(("zq",), zs.at[2, first], zq.at[first], zh_up, zq)
            push(("zq",), zs.at[2, second], zq.at[second], zh_dn, zq)
        elif i == 3:
            arrive(("zq",))
            zs[3, first] = part[3, pl.ds(0, half)].astype(BF16)
            zs[3, second] = (part[3, pl.ds(half, half)] + zq[second].astype(F32)).astype(BF16)
            push(("zr",), zs.at[3], zr.at[1], zh_dn, zr)

    def input_far():
        arrive(("zq",))
        zs[1, first] = (part[1, pl.ds(0, half)] + zq[first].astype(F32)).astype(BF16)
        push(("zr",), zs.at[1, first], zr.at[0, first], zh_up, zr)

    def input_out():
        arrive(("zr",))
        gout[...] = (
            part[0, at_y(0)] + zr[0].astype(F32) + zr[1].astype(F32)
        ).astype(BF16)
        move(6, gout, gin_hbm)

    scale = float(NY * chunk) ** -0.5

    def weight_rows(k, i):
        s = 0 if k < 2 else 1
        for pair in (0, 1):
            js = slice(2 * pair, 2 * pair + 2)
            if k < 2:
                left = az[i, js, :, k].reshape(4 * ffb, chunk)
            else:
                left = jnp.concatenate(
                    [ax[i, h, j] for j in (2 * pair, 2 * pair + 1) for h in (0, 1)], axis=0
                )
            for n in range(d_model // n_tile):
                cols = pl.ds(n * n_tile, n_tile)
                right = tg[i, :, :, s, :, cols].reshape(chunk, n_tile)
                out = mm(left, right, ((1,), (0,))).reshape(2, 2, ffb, n_tile)
                if i > 0:
                    out = out + acc[k, js, :, :, cols]
                if i < NY - 1:
                    acc[k, js, :, :, cols] = out
                else:
                    stage[k, js, :, :, cols] = (out * scale).astype(BF16)
            if i == NY - 1:
                out_hbm_k = (dg_hbm, du_hbm, dd_hbm)[k]
                for j in (2 * pair, 2 * pair + 1):
                    for h in range(2):
                        move(3 + k, stage.at[k, j, h], out_hbm_k.at[hbm_rows(j, h)])

    def weight_pair(i):
        weight_rows(0, i)
        weight_rows(1, i)

    def weight_down(i):
        arrive(("hz", i))
        weight_rows(2, i)

    gather_start()
    gather_far(0, 0)
    gather_far(0, 1)
    gather_twin(0, 0)
    gather_y(1, 0)
    gate_up_start(0)
    gather_z()
    gather_twin(0, 1)
    gather_far(1, 0)
    gather_y(1, 1)
    gather_y(3, 0)
    gather_twin(1, 0)
    gate_up_pass(0)
    gather_far(1, 1)
    hid_start(0)
    gate_up_start(1)
    gather_far(3, 0)
    gather_y(2, 0)
    gather_twin(1, 1)
    gate_up_pass(1)
    hid_start(1)
    gather_twin(3, 0)
    gather_far(2, 0)
    hid_cross(0)
    gate_up_start(3)
    gate_up_cross(1)
    gather_twin(2, 0)
    hid_cross(1)
    hid_start(3)
    gate_up_start(2)
    hid_pass(1)
    hid_start(2)
    gate_up_pass(2)
    gate_up_cross(0)
    gate_up_pass(3)
    pointwise(1)
    gate_up_cross(2)
    hid_pass(0)
    gate_up_cross(3)
    hid_cross(3)
    hid_cross(2)
    pointwise(0)
    hid_pass(2)
    hid_pass(3)
    spread_pair(1)
    pointwise(2)
    down_start(0)
    spread_pair(2)
    spread_far(1)
    input_near(1)
    down_start(1)
    spread_far(2)
    pointwise(3)
    input_near(2)
    spread_pair(3)
    down_far(0)
    input_rows(1)
    input_fold(1)
    down_start(3)
    input_rows(2)
    down_far(1)
    input_fold(2)
    input_pass(1)
    spread_far(3)
    down_last(0)
    input_pass(2)
    spread_pair(0)
    input_own(1)
    input_near(3)
    down_last(1)
    weight_down(0)
    input_own(2)
    input_rows(3)
    down_start(2)
    spread_far(0)
    down_far(3)
    input_fold(3)
    weight_down(1)
    down_far(2)
    input_near(0)
    input_far()
    input_pass(3)
    input_rows(0)
    weight_pair(0)
    input_own(3)
    down_last(2)
    input_fold(0)
    weight_pair(1)
    down_last(3)
    weight_pair(2)
    input_pass(0)
    weight_pair(3)
    weight_down(2)
    weight_down(3)
    input_own(0)
    input_out()
    assert arrived == set(groups)
    all_sent()
    for k in range(3):
        moved(3 + k, stage.at[k])
    moved(6, gout)


def hand_over(*refs):
    sems = refs[-1]
    inward, outward = [], []
    for n in (1, 2, 3, 0):
        src, dst, mid = refs[n], refs[4 + n], refs[8 + n]
        rows = src.shape[0]
        parts = HAND_PARTS if n else 1
        for p in range(parts):
            at = pl.ds(p * (rows // parts), rows // parts)
            inward.append(pltpu.make_async_copy(src.at[at], mid.at[at], sems.at[0, n, p]))
            outward.append(pltpu.make_async_copy(mid.at[at], dst.at[at], sems.at[1, n, p]))
    for copy in inward:
        copy.start()
    for arrived, copy in zip(inward, outward):
        arrived.wait()
        copy.start()
    for copy in outward:
        copy.wait()


def local(tokens, w_gate, w_up, w_down, grad_out):
    piece, d = tokens.shape
    ff = w_gate.shape[0]
    ffb, chunk = ff // 8, 8 * piece
    hbm = pl.BlockSpec(memory_space=pl.ANY)

    def vmem(*shape, dtype=BF16):
        return pltpu.VMEM(shape, dtype)

    scratch = [
        vmem(4, 2, 4, 2, piece, d),
        vmem(3, 4, 2, ffb, d),
        vmem(4, 4, 2, 2, ffb, chunk),
        vmem(4, 2, 2, ffb, chunk),
        vmem(4, 2, 2, 2, ffb, chunk),
        vmem(4, 2, ffb, chunk),
        vmem(4, 2, 4, ffb, chunk),
        vmem(4, 4, ffb, chunk),
        vmem(4, ffb, chunk),
        vmem(4, 2, ffb, chunk),
        vmem(4, 4, 2, 2, ffb, chunk),
        vmem(4, 2, 4, ffb, chunk),
        vmem(3, 4, 2, ffb, d, dtype=F32),
        vmem(3, 4, 2, ffb, d),
        vmem(2, 4, chunk, 2 * ffb),
        vmem(4, chunk, d, dtype=F32),
        vmem(4, chunk // 2, d),
        vmem(4, chunk // 2, d),
        vmem(4, 4, piece, d),
        vmem(4, piece, d),
        vmem(4, 2, piece, d),
        vmem(4, piece, d),
        vmem(piece, d),
        vmem(2, piece, d),
        vmem(piece, d),
        pltpu.SemaphoreType.DMA((26,)),
        pltpu.SemaphoreType.DMA((120,)),
        pltpu.SemaphoreType.DMA((8,)),
    ]
    weight = jax.ShapeDtypeStruct((ff, d), BF16)
    held = pl.pallas_call(
        body,
        out_shape=(jax.ShapeDtypeStruct((piece, d), BF16), weight, weight, weight),
        in_specs=[hbm] * 5,
        out_specs=(hbm,) * 4,
        scratch_shapes=scratch,
        compiler_params=pltpu.CompilerParams(
            collective_id=0, has_side_effects=True, vmem_limit_bytes=60 * 2 ** 20
        ),
        cost_estimate=pl.CostEstimate(
            flops=16 * 4 * chunk * ff * d, bytes_accessed=12 * ff * d, transcendentals=4 * chunk * ffb
        ),
    )(tokens, w_gate, w_up, w_down, grad_out)
    return pl.pallas_call(
        hand_over,
        out_shape=tuple(jax.ShapeDtypeStruct(one.shape, one.dtype) for one in held),
        in_specs=[hbm] * 4,
        out_specs=(hbm,) * 4,
        scratch_shapes=[vmem(*one.shape) for one in held] + [pltpu.SemaphoreType.DMA((2, 4, HAND_PARTS))],
        compiler_params=pltpu.CompilerParams(vmem_limit_bytes=60 * 2 ** 20),
        cost_estimate=pl.CostEstimate(flops=0, bytes_accessed=12 * ff * d, transcendentals=0),
    )(*held)


def solution(mesh):
    spec = P("row", "col")
    return jax.shard_map(
        local, mesh=mesh, in_specs=(spec,) * 5, out_specs=(spec,) * 4, check_vma=False
    )
```

```python
import jax
import jax.numpy as jnp
from jax import lax
from jax.experimental import pallas as pl
from jax.experimental.pallas import tpu as pltpu
from jax.sharding import PartitionSpec as P

NY, NZ, NX = 4, 4, 4
F32, BF16 = jnp.float32, jnp.bfloat16
HAND_PARTS = 1


def mm(a, b, dims):
    return lax.dot_general(a, b, (dims, ((), ())), preferred_element_type=F32)


def body(
    tok_hbm, wg_hbm, wu_hbm, wd_hbm, out_hbm,
    gin_hbm, dg_hbm, du_hbm, dd_hbm,
    tg, w, px, rxt, rxf, rz, pz, rzz, rzt, rzf, az, ax, acc, stage, trans,
    part, gs, gc, ys, yt, yf, zs, zq, zr, gout,
    send, recv, local,
):
    row, col = lax.axis_index("row"), lax.axis_index("col")
    y, zh, core = row // 8, (row // 2) % 4, row % 2
    zl, x = col // 4, col % 4

    def at_row(y_, zh_, core_):
        return {"row": (y_ * 4 + zh_) * 2 + core_, "col": col}

    def at_col(zl_, x_):
        return {"row": row, "col": zl_ * 4 + x_}

    y_up, y_dn = at_row((y + 1) % 4, zh, core), at_row((y + 3) % 4, zh, core)
    zh_up, zh_dn = at_row(y, (zh + 1) % 4, core), at_row(y, (zh + 3) % 4, core)
    twin = at_row(y, zh, 1 - core)
    x_up, x_dn = at_col(zl, (x + 1) % 4), at_col(zl, (x + 3) % 4)
    z_pair = at_col(1 - zl, x)
    partners = [y_up, y_dn, zh_up, zh_dn, twin, x_up, x_dn, z_pair]

    sends, groups, arrived = {}, {}, set()
    sent_refs = {
        "xt": rxt, "xf": rxf, "xz": rz, "zz": rzz, "zt": rzt, "zf": rzf,
        "gz": az.at[:, 0, 1], "gx0": az.at[:, 3], "gx1": az.at[:, 1], "gt": az.at[:, 2],
        "hx0": ax.at[:, 0, 3], "hx1": ax.at[:, 0, 1], "ht": ax.at[:, 0, 2], "hz": ax.at[:, 1],
        "cc": gc, "yt": yt, "yf": yf, "zq": zq, "zr": zr,
        "az1": tg.at[3, 0, 0], "az3": tg.at[1, 0, 0], "at": tg.at[2, 0, 0],
        "ay1": tg.at[:, 3, 0], "ay3": tg.at[:, 1, 0], "ax": tg.at[:, 2, 0], "ac": tg.at[:, :, 1],
    }

    def copy_of(src, dst, send_at, recv_at, device):
        return pltpu.make_async_remote_copy(
            src_ref=src, dst_ref=dst, send_sem=send.at[send_at], recv_sem=recv.at[recv_at],
            device_id=device, device_id_type=pl.DeviceIdType.MESH,
        )

    def push(key, src, dst, device, whole=None):
        send_at = sends.setdefault(key[0], len(sends))
        recv_at, _ = groups.setdefault(key, (len(groups), dst if whole is None else whole))
        copy_of(src, dst, send_at, recv_at, device).start()

    def arrive(*keys):
        for key in keys:
            if key not in arrived:
                arrived.add(key)
                recv_at, whole = groups[key]
                copy_of(whole, whole, 0, recv_at, twin).wait_recv()

    def all_sent():
        for kind, send_at in sends.items():
            copy_of(sent_refs[kind], sent_refs[kind], send_at, 0, twin).wait_send()

    def move(n, src, dst):
        copy = pltpu.make_async_copy(src, dst, local.at[n])
        copy.start()
        return copy

    def moved(n, whole):
        pltpu.make_async_copy(whole, whole, local.at[n]).wait()

    d_model = w.shape[-1]
    ffb = w.shape[-2]
    cut = -(-ffb // 32) * 16
    chunk = px.shape[-1]
    halves = (pl.ds(0, cut), pl.ds(cut, ffb - cut))
    n_tile = min(256, d_model)

    def hbm_rows(j, h):
        first = ((x + j) % 4) * (2 * ffb) + (zl if h == 0 else 1 - zl) * ffb
        return pl.ds(pl.multiple_of(first, 16), ffb)

    tok_in = [move(6, tok_hbm, tg.at[0, 0, 0, 0]), move(7, out_hbm, tg.at[0, 0, 0, 1])]
    for k, src in enumerate((wg_hbm, wu_hbm, wd_hbm)):
        for j in range(4):
            for h in range(2):
                move(k, src.at[hbm_rows(j, h)], w.at[k, j, h])

    barrier = pltpu.get_barrier_semaphore()
    for partner in partners:
        pl.semaphore_signal(barrier, inc=1, device_id=partner, device_id_type=pl.DeviceIdType.MESH)
    for copy in tok_in:
        copy.wait()
    pl.semaphore_wait(barrier, len(partners))

    half = chunk // 16
    first, second = pl.ds(0, half), pl.ds(half, half)
    both = pl.ds(0, 2)

    def gather_start():
        for s in (0, 1):
            own = tg.at[0, 0, 0, s]
            push(("ay1", 0, s), own, tg.at[0, 3, 0, s], y_up)
            push(("ay3", 0, s), own, tg.at[0, 1, 0, s], y_dn)
            push(("ac", 0, s, 0), own, tg.at[0, 0, 1, s], twin, tg.at[0, pl.ds(0, 2), 1, s])
            push(("az1", s), own, tg.at[3, 0, 0, s], zh_up)
            push(("az3", s), own, tg.at[1, 0, 0, s], zh_dn)

    def gather_z():
        arrive(("az1", 0), ("az1", 1))
        push(("at",), tg.at[3, 0, 0, :, first], tg.at[2, 0, 0, :, first], zh_up, tg.at[2, 0, 0])
        arrive(("az3", 0), ("az3", 1))
        push(("at",), tg.at[1, 0, 0, :, second], tg.at[2, 0, 0, :, second], zh_dn, tg.at[2, 0, 0])

    def kind(c, s):
        return s if c < 2 else both

    def gather_y(c, s):
        if c == 1:
            arrive(("az3", s))
        elif c == 3:
            arrive(("az1", 0), ("az1", 1))
        else:
            arrive(("at",))
        own = tg.at[c, 0, 0, kind(c, s)]
        push(("ay1", c, s), own, tg.at[c, 3, 0, kind(c, s)], y_up)
        push(("ay3", c, s), own, tg.at[c, 1, 0, kind(c, s)], y_dn)

    def gather_near(c, s):
        far = tg.at[c, 2, 0, kind(c, s)]
        arrive(("ay3", c, s))
        push(("ax", c, s), tg.at[c, 1, 0, kind(c, s), second], tg.at[c, 2, 0, kind(c, s), second], y_dn, far)
        if c == 0:
            push(("ac", 0, s, 0), tg.at[0, 1, 0, s], tg.at[0, 1, 1, s], twin, tg.at[0, pl.ds(0, 2), 1, s])

    def gather_far(c, s):
        far = tg.at[c, 2, 0, kind(c, s)]
        arrive(("ay1", c, s))
        push(("ax", c, s), tg.at[c, 3, 0, kind(c, s), first], tg.at[c, 2, 0, kind(c, s), first], y_up, far)
        if c == 0:
            push(("ac", 0, s, 1), tg.at[0, 3, 0, s], tg.at[0, 3, 1, s], twin, tg.at[0, pl.ds(2, 2), 1, s])
        else:
            gather_near(c, s)

    def gather_twin(c, s):
        arrive(("ax", c, s))
        if c == 0:
            push(("ac", 0, s, 1), tg.at[0, 2, 0, s], tg.at[0, 2, 1, s], twin, tg.at[0, pl.ds(2, 2), 1, s])
        else:
            push(("ac", c, s), tg.at[c, :, 0, kind(c, s)], tg.at[c, :, 1, kind(c, s)], twin)

    def gathered(s, c):
        if c == 0:
            arrive(("ac", 0, s, 0), ("ac", 0, s, 1))
        else:
            arrive(("ac", c, s if c < 2 else 0))

    def rows_of(s, c):
        return tg[c, :, :, s].reshape(chunk, d_model)

    def product(k, s, i, pair):
        part = w[k, 2 * pair:2 * pair + 2].reshape(4 * ffb, d_model)
        out = mm(part, rows_of(s, i), ((1,), (1,)))
        return out.astype(BF16).reshape(2, 2, ffb, chunk)

    def gate_up_first(part_at):
        if part_at == 0:
            moved(0, w.at[0])
            moved(1, w.at[1])
        arrive(("ac", 0, 0, part_at))
        lanes = pl.ds(part_at * (chunk // 2), chunk // 2)
        rows = tg[0, 2 * part_at:2 * part_at + 2, :, 0].reshape(chunk // 2, d_model)
        for pair in (1, 0):
            for k in (0, 1):
                weight = w[k, 2 * pair:2 * pair + 2].reshape(4 * ffb, d_model)
                out = mm(weight, rows, ((1,), (1,))).astype(BF16)
                px[0, 2 * pair:2 * pair + 2, :, k, :, lanes] = out.reshape(2, 2, ffb, chunk // 2)
            if pair == 1:
                push(("xt", 0), px.at[0, 2, 0, :, :, lanes], rxt.at[0, 0, :, :, lanes], x_up, rxt.at[0])
                push(("xt", 0), px.at[0, 2, 1, :, :, lanes], rxt.at[0, 1, :, :, lanes], x_dn, rxt.at[0])
                push(("xf", 0), px.at[0, 3, 0, :, :, lanes], rxf.at[0, 1, 0, :, :, lanes], x_dn, rxf.at[0])
            else:
                push(("xf", 0), px.at[0, 1, 1, :, :, lanes], rxf.at[0, 0, 1, :, :, lanes], x_up, rxf.at[0])

    def gate_up_start(i):
        gathered(0, i)
        for pair in (1, 0):
            for k in (0, 1):
                px[i, 2 * pair:2 * pair + 2, :, k] = product(k, 0, i, pair)
            if pair == 1:
                push(("xt", i), px.at[i, 2, 0], rxt.at[i, 0], x_up, rxt.at[i])
                push(("xt", i), px.at[i, 2, 1], rxt.at[i, 1], x_dn, rxt.at[i])
                push(("xf", i), px.at[i, 3, 0], rxf.at[i, 1, 0], x_dn, rxf.at[i])
            else:
                push(("xf", i), px.at[i, 1, 1], rxf.at[i, 0, 1], x_up, rxf.at[i])

    def gate_up_pass(i):
        arrive(("xt", i))
        px[i, 1, 0] = (px[i, 1, 0].astype(F32) + rxt[i, 0].astype(F32)).astype(BF16)
        push(("xf", i), px.at[i, 1, 0], rxf.at[i, 0, 0], x_up, rxf.at[i])
        px[i, 3, 1] = (px[i, 3, 1].astype(F32) + rxt[i, 1].astype(F32)).astype(BF16)
        push(("xf", i), px.at[i, 3, 1], rxf.at[i, 1, 1], x_dn, rxf.at[i])

    def gate_up_sum(i, h):
        return px[i, 0, h].astype(F32) + rxf[i, 0, h].astype(F32) + rxf[i, 1, h].astype(F32)

    def gate_up_cross(i):
        arrive(("xf", i))
        px[i, 0, 1] = gate_up_sum(i, 1).astype(BF16)
        push(("xz", i), px.at[i, 0, 1], rz.at[i], z_pair)

    def hid_start(i):
        if i == 0:
            moved(2, w.at[2])
        gathered(1, i)
        for pair in (1, 0):
            out = product(2, 1, i, pair)
            for j in range(2):
                for h in range(2):
                    pz[i, h, 2 * pair + j] = out[j, h]
        push(("zz", i), pz.at[i, 1], rzz.at[i], z_pair)

    def hid_cross(i):
        arrive(("zz", i))
        pz[i, 0] = (pz[i, 0].astype(F32) + rzz[i].astype(F32)).astype(BF16)
        for ab, (to, back, far, near) in enumerate(((x_up, x_dn, 0, 3), (x_dn, x_up, 1, 1))):
            push(("zt", i), pz.at[i, 0, 2, halves[ab]], rzt.at[i, halves[ab]], to, rzt.at[i])
        push(("zf", i), pz.at[i, 0, 3, halves[0]], rzf.at[i, 1, halves[0]], x_dn, rzf.at[i])
        push(("zf", i), pz.at[i, 0, 1, halves[1]], rzf.at[i, 0, halves[1]], x_up, rzf.at[i])

    def hid_pass(i):
        arrive(("zt", i))
        for ab, (j, to) in enumerate(((1, x_up), (3, x_dn))):
            part = pz[i, 0, j, halves[ab]].astype(F32) + rzt[i, halves[ab]].astype(F32)
            pz[i, 0, j, halves[ab]] = part.astype(BF16)
            push(("zf", i), pz.at[i, 0, j, halves[ab]], rzf.at[i, ab, halves[ab]], to, rzf.at[i])

    def pointwise(i):
        arrive(("xz", i))
        pre = gate_up_sum(i, 0) + rz[i].astype(F32)
        gate_pre, up_pre = pre[0], pre[1]
        arrive(("zf", i))
        hid_grad = pz[i, 0, 0].astype(F32) + rzf[i, 0].astype(F32) + rzf[i, 1].astype(F32)
        logistic = 1.0 / (1.0 + jnp.exp(-gate_pre))
        activated = gate_pre * logistic
        az[i, 0, 0, 0] = (hid_grad * up_pre * logistic * (1.0 + gate_pre * (1.0 - logistic))).astype(BF16)
        az[i, 0, 0, 1] = (hid_grad * activated).astype(BF16)
        push(("gz", i), az.at[i, 0, 0], az.at[i, 0, 1], z_pair)
        push(("gx0", i, 0), az.at[i, 0, 0], az.at[i, 3, 0], x_up)
        push(("gx1", i, 0), az.at[i, 0, 0], az.at[i, 1, 0], x_dn)
        ax[i, 0, 0] = (activated * up_pre).astype(BF16)

    def spread_pair(i):
        arrive(("gz", i))
        push(("gx0", i, 1), az.at[i, 0, 1], az.at[i, 3, 1], x_up)
        push(("gx1", i, 1), az.at[i, 0, 1], az.at[i, 1, 1], x_dn)

    def spread_far(i):
        arrive(("gx0", i, 0))
        push(("gt", i), az.at[i, 3, 0], az.at[i, 2, 0], x_up, az.at[i, 2])
        arrive(("gx1", i, 1))
        push(("gt", i), az.at[i, 1, 1], az.at[i, 2, 1], x_dn, az.at[i, 2])

    def down_start(i):
        push(("hx0", i), ax.at[i, 0, 0], ax.at[i, 0, 3], x_up)
        push(("hx1", i), ax.at[i, 0, 0], ax.at[i, 0, 1], x_dn)
        push(("hz", i), ax.at[i, 0, 0], ax.at[i, 1, 0], z_pair, ax.at[i, 1])

    def down_far(i):
        arrive(("hx0", i))
        push(("ht", i), ax.at[i, 0, 3, halves[0]], ax.at[i, 0, 2, halves[0]], x_up, ax.at[i, 0, 2])
        push(("hz", i), ax.at[i, 0, 3], ax.at[i, 1, 3], z_pair, ax.at[i, 1])
        arrive(("hx1", i))
        push(("ht", i), ax.at[i, 0, 1, halves[1]], ax.at[i, 0, 2, halves[1]], x_dn, ax.at[i, 0, 2])
        push(("hz", i), ax.at[i, 0, 1], ax.at[i, 1, 1], z_pair, ax.at[i, 1])

    def down_last(i):
        arrive(("ht", i))
        push(("hz", i), ax.at[i, 0, 2], ax.at[i, 1, 2], z_pair, ax.at[i, 1])

    def input_near(i):
        arrive(("gz", i), ("gx0", i, 0), ("gx1", i, 1), ("gx1", i, 0), ("gx0", i, 1))
        for j in (0, 1, 3):
            for k in (0, 1):
                trans[k, j] = az[i, j, :, k].reshape(2 * ffb, chunk).T
        for n in range(d_model // n_tile):
            cols = pl.ds(n * n_tile, n_tile)
            part[i, :, cols] = sum(
                mm(trans[k, j], w[k, j, :, :, cols].reshape(2 * ffb, n_tile), ((1,), (0,)))
                for k in (0, 1) for j in (0, 1, 3)
            )

    def input_rows(i):
        arrive(("gt", i))
        for k in (0, 1):
            trans[k, 2] = az[i, 2, :, k].reshape(2 * ffb, chunk).T
        for n in range(d_model // n_tile):
            cols = pl.ds(n * n_tile, n_tile)
            out = part[i, :, cols] + sum(
                mm(trans[k, 2], w[k, 2, :, :, cols].reshape(2 * ffb, n_tile), ((1,), (0,)))
                for k in (0, 1)
            )
            part[i, :, cols] = out
            other = out.reshape(4, 2, piece, n_tile)[:, 1].reshape(chunk // 2, n_tile)
            gs[i, :, cols] = other.astype(BF16)
        push(("cc", i), gs.at[i], gc.at[i], twin)

    piece = chunk // 8

    def at_y(yr):
        return pl.ds(yr * 2 * piece, piece)

    def at_other(yr):
        return pl.ds(yr * piece, piece)

    def input_fold(i):
        arrive(("cc", i))
        part[i, at_y(0)] = part[i, at_y(0)] + gc[i, at_other(0)].astype(F32)
        for yr in (2, 1, 3):
            ys[i, yr] = (part[i, at_y(yr)] + gc[i, at_other(yr)].astype(F32)).astype(BF16)
            if yr == 2:
                push(("yt", i), ys.at[i, 2, first], yt.at[i, first], y_up, yt.at[i])
                push(("yt", i), ys.at[i, 2, second], yt.at[i, second], y_dn, yt.at[i])
            elif yr == 1:
                push(("yf", i), ys.at[i, 1, second], yf.at[i, 0, second], y_up, yf.at[i])
            else:
                push(("yf", i), ys.at[i, 3, first], yf.at[i, 1, first], y_dn, yf.at[i])

    def input_pass(i):
        arrive(("yt", i))
        for ab, (yr, rows, to) in enumerate(((1, first, y_up), (3, second, y_dn))):
            ys[i, yr, rows] = (ys[i, yr, rows].astype(F32) + yt[i, rows].astype(F32)).astype(BF16)
            push(("yf", i), ys.at[i, yr, rows], yf.at[i, ab, rows], to, yf.at[i])

    def input_own(i):
        arrive(("yf", i))
        part[i, at_y(0)] = part[i, at_y(0)] + yf[i, 0].astype(F32) + yf[i, 1].astype(F32)
        if i == 1:
            zs[1, second] = part[1, pl.ds(half, half)].astype(BF16)
            push(("zr",), zs.at[1, second], zr.at[0, second], zh_up, zr)
        elif i == 2:
            zs[2] = part[2, at_y(0)].astype(BF16)
            push(("zq",), zs.at[2, first], zq.at[first], zh_up, zq)
            push(("zq",), zs.at[2, second], zq.at[second], zh_dn, zq)
        elif i == 3:
            arrive(("zq",))
            zs[3, first] = part[3, pl.ds(0, half)].astype(BF16)
            zs[3, second] = (part[3, pl.ds(half, half)] + zq[second].astype(F32)).astype(BF16)
            push(("zr",), zs.at[3], zr.at[1], zh_dn, zr)

    def input_far():
        arrive(("zq",))
        zs[1, first] = (part[1, pl.ds(0, half)] + zq[first].astype(F32)).astype(BF16)
        push(("zr",), zs.at[1, first], zr.at[0, first], zh_up, zr)

    def input_out():
        arrive(("zr",))
        gout[...] = (
            part[0, at_y(0)] + zr[0].astype(F32) + zr[1].astype(F32)
        ).astype(BF16)
        move(6, gout, gin_hbm)

    scale = float(NY * chunk) ** -0.5

    added = [0, 0, 0]

    def weight_rows(k, i):
        added[k] += 1
        s = 0 if k < 2 else 1
        for pair in (0, 1):
            js = slice(2 * pair, 2 * pair + 2)
            if k < 2:
                left = az[i, js, :, k].reshape(4 * ffb, chunk)
            else:
                left = jnp.concatenate(
                    [ax[i, h, j] for j in (2 * pair, 2 * pair + 1) for h in (0, 1)], axis=0
                )
            for n in range(d_model // n_tile):
                cols = pl.ds(n * n_tile, n_tile)
                right = tg[i, :, :, s, :, cols].reshape(chunk, n_tile)
                out = mm(left, right, ((1,), (0,))).reshape(2, 2, ffb, n_tile)
                if added[k] > 1:
                    out = out + acc[k, js, :, :, cols]
                if added[k] < NY:
                    acc[k, js, :, :, cols] = out
                else:
                    stage[k, js, :, :, cols] = (out * scale).astype(BF16)
            if added[k] == NY:
                out_hbm_k = (dg_hbm, du_hbm, dd_hbm)[k]
                for j in (2 * pair, 2 * pair + 1):
                    for h in range(2):
                        move(3 + k, stage.at[k, j, h], out_hbm_k.at[hbm_rows(j, h)])

    def weight_pair(i):
        weight_rows(0, i)
        weight_rows(1, i)

    def weight_down(i):
        arrive(("hz", i))
        weight_rows(2, i)

    gather_start()
    gather_near(0, 0)
    gather_far(0, 0)
    gate_up_first(0)
    gather_y(1, 0)
    gather_twin(0, 0)
    gather_far(0, 1)
    gather_near(0, 1)
    gate_up_first(1)
    gather_far(1, 0)
    gather_y(1, 1)
    gather_twin(0, 1)
    gate_up_pass(0)
    gather_y(3, 0)
    gather_z()
    gather_twin(1, 0)
    hid_start(0)
    gate_up_start(1)
    gather_far(1, 1)
    gather_far(3, 0)
    gather_twin(1, 1)
    gather_y(2, 0)
    gate_up_pass(1)
    gather_twin(3, 0)
    hid_start(1)
    hid_cross(0)
    gate_up_start(3)
    gather_far(2, 0)
    gate_up_cross(1)
    hid_start(3)
    gather_twin(2, 0)
    gate_up_pass(3)
    hid_cross(1)
    gate_up_start(2)
    hid_pass(1)
    hid_start(2)
    gate_up_pass(2)
    pointwise(1)
    gate_up_cross(0)
    hid_cross(2)
    gate_up_cross(2)
    hid_cross(3)
    gate_up_cross(3)
    spread_pair(1)
    hid_pass(3)
    hid_pass(2)
    down_start(1)
    spread_far(1)
    pointwise(2)
    pointwise(3)
    input_near(1)
    spread_pair(2)
    down_start(3)
    down_far(1)
    input_rows(1)
    hid_pass(0)
    input_fold(1)
    spread_far(2)
    spread_pair(3)
    pointwise(0)
    input_near(2)
    input_rows(2)
    input_pass(1)
    down_far(3)
    input_fold(2)
    down_start(0)
    spread_far(3)
    spread_pair(0)
    weight_pair(2)
    input_own(1)
    down_start(2)
    down_last(1)
    input_pass(2)
    weight_pair(1)
    input_near(3)
    input_own(2)
    down_last(3)
    input_rows(3)
    weight_pair(3)
    spread_far(0)
    down_far(0)
    input_fold(3)
    down_far(2)
    input_near(0)
    input_pass(3)
    input_rows(0)
    down_last(0)
    down_last(2)
    input_own(3)
    input_far()
    input_fold(0)
    weight_pair(0)
    weight_down(3)
    weight_down(1)
    input_pass(0)
    weight_down(2)
    weight_down(0)
    input_own(0)
    input_out()
    assert arrived == set(groups)
    all_sent()
    for k in range(3):
        moved(3 + k, stage.at[k])
    moved(6, gout)


def hand_over(*refs):
    sems = refs[-1]
    inward, outward = [], []
    for n in (1, 2, 3, 0):
        src, dst, mid = refs[n], refs[4 + n], refs[8 + n]
        rows = src.shape[0]
        parts = HAND_PARTS if n else 1
        for p in range(parts):
            at = pl.ds(p * (rows // parts), rows // parts)
            inward.append(pltpu.make_async_copy(src.at[at], mid.at[at], sems.at[0, n, p]))
            outward.append(pltpu.make_async_copy(mid.at[at], dst.at[at], sems.at[1, n, p]))
    for copy in inward:
        copy.start()
    for arrived, copy in zip(inward, outward):
        arrived.wait()
        copy.start()
    for copy in outward:
        copy.wait()


def local(tokens, w_gate, w_up, w_down, grad_out):
    piece, d = tokens.shape
    ff = w_gate.shape[0]
    ffb, chunk = ff // 8, 8 * piece
    hbm = pl.BlockSpec(memory_space=pl.ANY)

    def vmem(*shape, dtype=BF16):
        return pltpu.VMEM(shape, dtype)

    scratch = [
        vmem(4, 4, 2, 2, piece, d),
        vmem(3, 4, 2, ffb, d),
        vmem(4, 4, 2, 2, ffb, chunk),
        vmem(4, 2, 2, ffb, chunk),
        vmem(4, 2, 2, 2, ffb, chunk),
        vmem(4, 2, ffb, chunk),
        vmem(4, 2, 4, ffb, chunk),
        vmem(4, 4, ffb, chunk),
        vmem(4, ffb, chunk),
        vmem(4, 2, ffb, chunk),
        vmem(4, 4, 2, 2, ffb, chunk),
        vmem(4, 2, 4, ffb, chunk),
        vmem(3, 4, 2, ffb, d, dtype=F32),
        vmem(3, 4, 2, ffb, d),
        vmem(2, 4, chunk, 2 * ffb),
        vmem(4, chunk, d, dtype=F32),
        vmem(4, chunk // 2, d),
        vmem(4, chunk // 2, d),
        vmem(4, 4, piece, d),
        vmem(4, piece, d),
        vmem(4, 2, piece, d),
        vmem(4, piece, d),
        vmem(piece, d),
        vmem(2, piece, d),
        vmem(piece, d),
        pltpu.SemaphoreType.DMA((26,)),
        pltpu.SemaphoreType.DMA((120,)),
        pltpu.SemaphoreType.DMA((8,)),
    ]
    weight = jax.ShapeDtypeStruct((ff, d), BF16)
    held = pl.pallas_call(
        body,
        out_shape=(jax.ShapeDtypeStruct((piece, d), BF16), weight, weight, weight),
        in_specs=[hbm] * 5,
        out_specs=(hbm,) * 4,
        scratch_shapes=scratch,
        compiler_params=pltpu.CompilerParams(
            collective_id=0, has_side_effects=True, vmem_limit_bytes=60 * 2 ** 20
        ),
        cost_estimate=pl.CostEstimate(
            flops=16 * 4 * chunk * ff * d, bytes_accessed=12 * ff * d, transcendentals=4 * chunk * ffb
        ),
    )(tokens, w_gate, w_up, w_down, grad_out)
    return pl.pallas_call(
        hand_over,
        out_shape=tuple(jax.ShapeDtypeStruct(one.shape, one.dtype) for one in held),
        in_specs=[hbm] * 4,
        out_specs=(hbm,) * 4,
        scratch_shapes=[vmem(*one.shape) for one in held] + [pltpu.SemaphoreType.DMA((2, 4, HAND_PARTS))],
        compiler_params=pltpu.CompilerParams(vmem_limit_bytes=60 * 2 ** 20),
        cost_estimate=pl.CostEstimate(flops=0, bytes_accessed=12 * ff * d, transcendentals=0),
    )(*held)


def solution(mesh):
    spec = P("row", "col")
    return jax.shard_map(
        local, mesh=mesh, in_specs=(spec,) * 5, out_specs=(spec,) * 4, check_vma=False
    )
```

```python
import jax
import jax.numpy as jnp
from jax import lax
from jax.experimental import pallas as pl
from jax.experimental.pallas import tpu as pltpu
from jax.sharding import PartitionSpec as P

NY, NZ, NX = 4, 4, 4
F32, BF16 = jnp.float32, jnp.bfloat16
HAND_PARTS = 1


def mm(a, b, dims):
    return lax.dot_general(a, b, (dims, ((), ())), preferred_element_type=F32)


def body(
    tok_hbm, wg_hbm, wu_hbm, wd_hbm, out_hbm,
    gin_hbm, dg_hbm, du_hbm, dd_hbm,
    tg, w, px, rxt, rxf, rz, pz, rzz, rzt, rzf, az, ax, acc, stage, trans,
    part, gs, gc, ys, yt, yf, zs, zq, zr, gout,
    send, recv, local,
):
    row, col = lax.axis_index("row"), lax.axis_index("col")
    y, zh, core = row // 8, (row // 2) % 4, row % 2
    zl, x = col // 4, col % 4

    def at_row(y_, zh_, core_):
        return {"row": (y_ * 4 + zh_) * 2 + core_, "col": col}

    def at_col(zl_, x_):
        return {"row": row, "col": zl_ * 4 + x_}

    y_up, y_dn = at_row((y + 1) % 4, zh, core), at_row((y + 3) % 4, zh, core)
    zh_up, zh_dn = at_row(y, (zh + 1) % 4, core), at_row(y, (zh + 3) % 4, core)
    twin = at_row(y, zh, 1 - core)
    x_up, x_dn = at_col(zl, (x + 1) % 4), at_col(zl, (x + 3) % 4)
    z_pair = at_col(1 - zl, x)
    partners = [y_up, y_dn, zh_up, zh_dn, twin, x_up, x_dn, z_pair]

    sends, groups, arrived = {}, {}, set()
    sent_refs = {
        "xt": rxt, "xf": rxf, "xz": rz, "zz": rzz, "zt": rzt, "zf": rzf,
        "gz": az.at[:, 0, 1], "gx0": az.at[:, 3], "gx1": az.at[:, 1], "gt": az.at[:, 2],
        "hx0": ax.at[:, 0, 3], "hx1": ax.at[:, 0, 1], "ht": ax.at[:, 0, 2], "hz": ax.at[:, 1],
        "cc": gc, "yt": yt, "yf": yf, "zq": zq, "zr": zr,
        "az1": tg.at[3, 0, 0], "az3": tg.at[1, 0, 0], "at": tg.at[2, 0, 0],
        "ay1": tg.at[:, 3, 0], "ay3": tg.at[:, 1, 0], "ax": tg.at[:, 2, 0], "ac": tg.at[:, :, 1],
    }

    def copy_of(src, dst, send_at, recv_at, device):
        return pltpu.make_async_remote_copy(
            src_ref=src, dst_ref=dst, send_sem=send.at[send_at], recv_sem=recv.at[recv_at],
            device_id=device, device_id_type=pl.DeviceIdType.MESH,
        )

    def push(key, src, dst, device, whole=None):
        send_at = sends.setdefault(key[0], len(sends))
        recv_at, _ = groups.setdefault(key, (len(groups), dst if whole is None else whole))
        copy_of(src, dst, send_at, recv_at, device).start()

    def arrive(*keys):
        for key in keys:
            if key not in arrived:
                arrived.add(key)
                recv_at, whole = groups[key]
                copy_of(whole, whole, 0, recv_at, twin).wait_recv()

    def all_sent():
        for kind, send_at in sends.items():
            copy_of(sent_refs[kind], sent_refs[kind], send_at, 0, twin).wait_send()

    def move(n, src, dst):
        copy = pltpu.make_async_copy(src, dst, local.at[n])
        copy.start()
        return copy

    def moved(n, whole):
        pltpu.make_async_copy(whole, whole, local.at[n]).wait()

    d_model = w.shape[-1]
    ffb = w.shape[-2]
    cut = -(-ffb // 32) * 16
    chunk = px.shape[-1]
    halves = (pl.ds(0, cut), pl.ds(cut, ffb - cut))
    n_tile = min(256, d_model)

    def hbm_rows(j, h):
        first = ((x + j) % 4) * (2 * ffb) + (zl if h == 0 else 1 - zl) * ffb
        return pl.ds(pl.multiple_of(first, 16), ffb)

    tok_in = [move(6, tok_hbm, tg.at[0, 0, 0, 0]), move(7, out_hbm, tg.at[0, 0, 0, 1])]
    for k, src in enumerate((wg_hbm, wu_hbm, wd_hbm)):
        for j in range(4):
            for h in range(2):
                move(k, src.at[hbm_rows(j, h)], w.at[k, j, h])

    barrier = pltpu.get_barrier_semaphore()
    for partner in partners:
        pl.semaphore_signal(barrier, inc=1, device_id=partner, device_id_type=pl.DeviceIdType.MESH)
    for copy in tok_in:
        copy.wait()
    pl.semaphore_wait(barrier, len(partners))

    half = chunk // 16
    first, second = pl.ds(0, half), pl.ds(half, half)
    both = pl.ds(0, 2)

    def gather_start():
        for s in (0, 1):
            own = tg.at[0, 0, 0, s]
            push(("ay1", 0, s), own, tg.at[0, 3, 0, s], y_up)
            push(("ay3", 0, s), own, tg.at[0, 1, 0, s], y_dn)
            push(("ac", 0, s, 0), own, tg.at[0, 0, 1, s], twin, tg.at[0, pl.ds(0, 2), 1, s])
            push(("az1", s), own, tg.at[3, 0, 0, s], zh_up)
            push(("az3", s), own, tg.at[1, 0, 0, s], zh_dn)

    def gather_z():
        arrive(("az1", 0), ("az1", 1))
        push(("at",), tg.at[3, 0, 0, :, first], tg.at[2, 0, 0, :, first], zh_up, tg.at[2, 0, 0])
        arrive(("az3", 0), ("az3", 1))
        push(("at",), tg.at[1, 0, 0, :, second], tg.at[2, 0, 0, :, second], zh_dn, tg.at[2, 0, 0])

    def kind(c, s):
        return s if c < 2 else both

    def gather_y(c, s):
        if c == 1:
            arrive(("az3", s))
        elif c == 3:
            arrive(("az1", 0), ("az1", 1))
        else:
            arrive(("at",))
        own = tg.at[c, 0, 0, kind(c, s)]
        push(("ay1", c, s), own, tg.at[c, 3, 0, kind(c, s)], y_up)
        push(("ay3", c, s), own, tg.at[c, 1, 0, kind(c, s)], y_dn)

    def gather_near(c, s):
        far = tg.at[c, 2, 0, kind(c, s)]
        arrive(("ay3", c, s))
        push(("ax", c, s), tg.at[c, 1, 0, kind(c, s), second], tg.at[c, 2, 0, kind(c, s), second], y_dn, far)
        if c == 0:
            push(("ac", 0, s, 0), tg.at[0, 1, 0, s], tg.at[0, 1, 1, s], twin, tg.at[0, pl.ds(0, 2), 1, s])

    def gather_far(c, s):
        far = tg.at[c, 2, 0, kind(c, s)]
        arrive(("ay1", c, s))
        push(("ax", c, s), tg.at[c, 3, 0, kind(c, s), first], tg.at[c, 2, 0, kind(c, s), first], y_up, far)
        if c == 0:
            push(("ac", 0, s, 1), tg.at[0, 3, 0, s], tg.at[0, 3, 1, s], twin, tg.at[0, pl.ds(2, 2), 1, s])
        else:
            gather_near(c, s)

    def gather_twin(c, s):
        arrive(("ax", c, s))
        if c == 0:
            push(("ac", 0, s, 1), tg.at[0, 2, 0, s], tg.at[0, 2, 1, s], twin, tg.at[0, pl.ds(2, 2), 1, s])
        else:
            push(("ac", c, s), tg.at[c, :, 0, kind(c, s)], tg.at[c, :, 1, kind(c, s)], twin)

    def gathered(s, c):
        if c == 0:
            arrive(("ac", 0, s, 0), ("ac", 0, s, 1))
        else:
            arrive(("ac", c, s if c < 2 else 0))

    def rows_of(s, c):
        return tg[c, :, :, s].reshape(chunk, d_model)

    def product(k, s, i, pair):
        part = w[k, 2 * pair:2 * pair + 2].reshape(4 * ffb, d_model)
        out = mm(part, rows_of(s, i), ((1,), (1,)))
        return out.astype(BF16).reshape(2, 2, ffb, chunk)

    def gate_up_first(part_at):
        if part_at == 0:
            moved(0, w.at[0])
            moved(1, w.at[1])
        arrive(("ac", 0, 0, part_at))
        lanes = pl.ds(part_at * (chunk // 2), chunk // 2)
        rows = tg[0, 2 * part_at:2 * part_at + 2, :, 0].reshape(chunk // 2, d_model)
        for pair in (1, 0):
            for k in (0, 1):
                weight = w[k, 2 * pair:2 * pair + 2].reshape(4 * ffb, d_model)
                out = mm(weight, rows, ((1,), (1,))).astype(BF16)
                px[0, 2 * pair:2 * pair + 2, :, k, :, lanes] = out.reshape(2, 2, ffb, chunk // 2)
            if pair == 1:
                push(("xt", 0), px.at[0, 2, 0, :, :, lanes], rxt.at[0, 0, :, :, lanes], x_up, rxt.at[0])
                push(("xt", 0), px.at[0, 2, 1, :, :, lanes], rxt.at[0, 1, :, :, lanes], x_dn, rxt.at[0])
                push(("xf", 0), px.at[0, 3, 0, :, :, lanes], rxf.at[0, 1, 0, :, :, lanes], x_dn, rxf.at[0])
            else:
                push(("xf", 0), px.at[0, 1, 1, :, :, lanes], rxf.at[0, 0, 1, :, :, lanes], x_up, rxf.at[0])

    def gate_up_start(i):
        gathered(0, i)
        for pair in (1, 0):
            for k in (0, 1):
                px[i, 2 * pair:2 * pair + 2, :, k] = product(k, 0, i, pair)
            if pair == 1:
                push(("xt", i), px.at[i, 2, 0], rxt.at[i, 0], x_up, rxt.at[i])
                push(("xt", i), px.at[i, 2, 1], rxt.at[i, 1], x_dn, rxt.at[i])
                push(("xf", i), px.at[i, 3, 0], rxf.at[i, 1, 0], x_dn, rxf.at[i])
            else:
                push(("xf", i), px.at[i, 1, 1], rxf.at[i, 0, 1], x_up, rxf.at[i])

    def gate_up_pass(i):
        arrive(("xt", i))
        px[i, 1, 0] = (px[i, 1, 0].astype(F32) + rxt[i, 0].astype(F32)).astype(BF16)
        push(("xf", i), px.at[i, 1, 0], rxf.at[i, 0, 0], x_up, rxf.at[i])
        px[i, 3, 1] = (px[i, 3, 1].astype(F32) + rxt[i, 1].astype(F32)).astype(BF16)
        push(("xf", i), px.at[i, 3, 1], rxf.at[i, 1, 1], x_dn, rxf.at[i])

    def gate_up_sum(i, h):
        return px[i, 0, h].astype(F32) + rxf[i, 0, h].astype(F32) + rxf[i, 1, h].astype(F32)

    def gate_up_cross(i):
        arrive(("xf", i))
        px[i, 0, 1] = gate_up_sum(i, 1).astype(BF16)
        push(("xz", i), px.at[i, 0, 1], rz.at[i], z_pair)

    def hid_start(i):
        if i == 0:
            moved(2, w.at[2])
        gathered(1, i)
        for pair in (1, 0):
            out = product(2, 1, i, pair)
            for j in range(2):
                for h in range(2):
                    pz[i, h, 2 * pair + j] = out[j, h]
        push(("zz", i), pz.at[i, 1], rzz.at[i], z_pair)

    def hid_cross(i):
        arrive(("zz", i))
        pz[i, 0] = (pz[i, 0].astype(F32) + rzz[i].astype(F32)).astype(BF16)
        for ab, (to, back, far, near) in enumerate(((x_up, x_dn, 0, 3), (x_dn, x_up, 1, 1))):
            push(("zt", i), pz.at[i, 0, 2, halves[ab]], rzt.at[i, halves[ab]], to, rzt.at[i])
        push(("zf", i), pz.at[i, 0, 3, halves[0]], rzf.at[i, 1, halves[0]], x_dn, rzf.at[i])
        push(("zf", i), pz.at[i, 0, 1, halves[1]], rzf.at[i, 0, halves[1]], x_up, rzf.at[i])

    def hid_pass(i):
        arrive(("zt", i))
        for ab, (j, to) in enumerate(((1, x_up), (3, x_dn))):
            part = pz[i, 0, j, halves[ab]].astype(F32) + rzt[i, halves[ab]].astype(F32)
            pz[i, 0, j, halves[ab]] = part.astype(BF16)
            push(("zf", i), pz.at[i, 0, j, halves[ab]], rzf.at[i, ab, halves[ab]], to, rzf.at[i])

    def pointwise(i):
        arrive(("xz", i))
        pre = gate_up_sum(i, 0) + rz[i].astype(F32)
        gate_pre, up_pre = pre[0], pre[1]
        arrive(("zf", i))
        hid_grad = pz[i, 0, 0].astype(F32) + rzf[i, 0].astype(F32) + rzf[i, 1].astype(F32)
        logistic = 1.0 / (1.0 + jnp.exp(-gate_pre))
        activated = gate_pre * logistic
        az[i, 0, 0, 0] = (hid_grad * up_pre * logistic * (1.0 + gate_pre * (1.0 - logistic))).astype(BF16)
        az[i, 0, 0, 1] = (hid_grad * activated).astype(BF16)
        push(("gz", i), az.at[i, 0, 0], az.at[i, 0, 1], z_pair)
        push(("gx0", i, 0), az.at[i, 0, 0], az.at[i, 3, 0], x_up)
        push(("gx1", i, 0), az.at[i, 0, 0], az.at[i, 1, 0], x_dn)
        ax[i, 0, 0] = (activated * up_pre).astype(BF16)

    def spread_pair(i):
        arrive(("gz", i))
        push(("gx0", i, 1), az.at[i, 0, 1], az.at[i, 3, 1], x_up)
        push(("gx1", i, 1), az.at[i, 0, 1], az.at[i, 1, 1], x_dn)

    def spread_far(i):
        arrive(("gx0", i, 0))
        push(("gt", i), az.at[i, 3, 0], az.at[i, 2, 0], x_up, az.at[i, 2])
        arrive(("gx1", i, 1))
        push(("gt", i), az.at[i, 1, 1], az.at[i, 2, 1], x_dn, az.at[i, 2])

    def down_start(i):
        push(("hx0", i), ax.at[i, 0, 0], ax.at[i, 0, 3], x_up)
        push(("hx1", i), ax.at[i, 0, 0], ax.at[i, 0, 1], x_dn)
        push(("hz", i), ax.at[i, 0, 0], ax.at[i, 1, 0], z_pair, ax.at[i, 1])

    def down_far(i):
        arrive(("hx0", i))
        push(("ht", i), ax.at[i, 0, 3, halves[0]], ax.at[i, 0, 2, halves[0]], x_up, ax.at[i, 0, 2])
        push(("hz", i), ax.at[i, 0, 3], ax.at[i, 1, 3], z_pair, ax.at[i, 1])
        arrive(("hx1", i))
        push(("ht", i), ax.at[i, 0, 1, halves[1]], ax.at[i, 0, 2, halves[1]], x_dn, ax.at[i, 0, 2])
        push(("hz", i), ax.at[i, 0, 1], ax.at[i, 1, 1], z_pair, ax.at[i, 1])

    def down_last(i):
        arrive(("ht", i))
        push(("hz", i), ax.at[i, 0, 2], ax.at[i, 1, 2], z_pair, ax.at[i, 1])

    def input_near(i):
        arrive(("gz", i), ("gx0", i, 0), ("gx1", i, 1), ("gx1", i, 0), ("gx0", i, 1))
        for j in (0, 1, 3):
            for k in (0, 1):
                trans[k, j] = az[i, j, :, k].reshape(2 * ffb, chunk).T
        for n in range(d_model // n_tile):
            cols = pl.ds(n * n_tile, n_tile)
            part[i, :, cols] = sum(
                mm(trans[k, j], w[k, j, :, :, cols].reshape(2 * ffb, n_tile), ((1,), (0,)))
                for k in (0, 1) for j in (0, 1, 3)
            )

    def input_rows(i):
        arrive(("gt", i))
        for k in (0, 1):
            trans[k, 2] = az[i, 2, :, k].reshape(2 * ffb, chunk).T
        for n in range(d_model // n_tile):
            cols = pl.ds(n * n_tile, n_tile)
            out = part[i, :, cols] + sum(
                mm(trans[k, 2], w[k, 2, :, :, cols].reshape(2 * ffb, n_tile), ((1,), (0,)))
                for k in (0, 1)
            )
            part[i, :, cols] = out
            other = out.reshape(4, 2, piece, n_tile)[:, 1].reshape(chunk // 2, n_tile)
            gs[i, :, cols] = other.astype(BF16)
        push(("cc", i), gs.at[i], gc.at[i], twin)

    piece = chunk // 8

    def at_y(yr):
        return pl.ds(yr * 2 * piece, piece)

    def at_other(yr):
        return pl.ds(yr * piece, piece)

    def input_fold(i):
        arrive(("cc", i))
        part[i, at_y(0)] = part[i, at_y(0)] + gc[i, at_other(0)].astype(F32)
        for yr in (2, 1, 3):
            ys[i, yr] = (part[i, at_y(yr)] + gc[i, at_other(yr)].astype(F32)).astype(BF16)
            if yr == 2:
                push(("yt", i), ys.at[i, 2, first], yt.at[i, first], y_up, yt.at[i])
                push(("yt", i), ys.at[i, 2, second], yt.at[i, second], y_dn, yt.at[i])
            elif yr == 1:
                push(("yf", i), ys.at[i, 1, second], yf.at[i, 0, second], y_up, yf.at[i])
            else:
                push(("yf", i), ys.at[i, 3, first], yf.at[i, 1, first], y_dn, yf.at[i])

    def input_pass(i):
        arrive(("yt", i))
        for ab, (yr, rows, to) in enumerate(((1, first, y_up), (3, second, y_dn))):
            ys[i, yr, rows] = (ys[i, yr, rows].astype(F32) + yt[i, rows].astype(F32)).astype(BF16)
            push(("yf", i), ys.at[i, yr, rows], yf.at[i, ab, rows], to, yf.at[i])

    def input_own(i):
        arrive(("yf", i))
        part[i, at_y(0)] = part[i, at_y(0)] + yf[i, 0].astype(F32) + yf[i, 1].astype(F32)
        if i == 1:
            zs[1, second] = part[1, pl.ds(half, half)].astype(BF16)
            push(("zr",), zs.at[1, second], zr.at[0, second], zh_up, zr)
        elif i == 2:
            zs[2] = part[2, at_y(0)].astype(BF16)
            push(("zq",), zs.at[2, first], zq.at[first], zh_up, zq)
            push(("zq",), zs.at[2, second], zq.at[second], zh_dn, zq)
        elif i == 3:
            arrive(("zq",))
            zs[3, first] = part[3, pl.ds(0, half)].astype(BF16)
            zs[3, second] = (part[3, pl.ds(half, half)] + zq[second].astype(F32)).astype(BF16)
            push(("zr",), zs.at[3], zr.at[1], zh_dn, zr)

    def input_far():
        arrive(("zq",))
        zs[1, first] = (part[1, pl.ds(0, half)] + zq[first].astype(F32)).astype(BF16)
        push(("zr",), zs.at[1, first], zr.at[0, first], zh_up, zr)

    def input_out():
        arrive(("zr",))
        gout[...] = (
            part[0, at_y(0)] + zr[0].astype(F32) + zr[1].astype(F32)
        ).astype(BF16)
        move(6, gout, gin_hbm)

    scale = float(NY * chunk) ** -0.5

    added = [0, 0, 0]

    def weight_rows(k, i):
        added[k] += 1
        s = 0 if k < 2 else 1
        for pair in (0, 1):
            js = slice(2 * pair, 2 * pair + 2)
            if k < 2:
                left = az[i, js, :, k].reshape(4 * ffb, chunk)
            else:
                left = jnp.concatenate(
                    [ax[i, h, j] for j in (2 * pair, 2 * pair + 1) for h in (0, 1)], axis=0
                )
            for n in range(d_model // n_tile):
                cols = pl.ds(n * n_tile, n_tile)
                right = tg[i, :, :, s, :, cols].reshape(chunk, n_tile)
                out = mm(left, right, ((1,), (0,))).reshape(2, 2, ffb, n_tile)
                if added[k] > 1:
                    out = out + acc[k, js, :, :, cols]
                if added[k] < NY:
                    acc[k, js, :, :, cols] = out
                else:
                    stage[k, js, :, :, cols] = (out * scale).astype(BF16)
            if added[k] == NY:
                out_hbm_k = (dg_hbm, du_hbm, dd_hbm)[k]
                for j in (2 * pair, 2 * pair + 1):
                    for h in range(2):
                        move(3 + k, stage.at[k, j, h], out_hbm_k.at[hbm_rows(j, h)])

    def weight_pair(i):
        weight_rows(0, i)
        weight_rows(1, i)

    def weight_down(i):
        arrive(("hz", i))
        weight_rows(2, i)

    gather_start()
    gather_near(0, 0)
    gather_far(0, 0)
    gather_far(0, 1)
    gather_near(0, 1)
    gate_up_first(0)
    gather_y(1, 0)
    gather_twin(0, 0)
    gather_twin(0, 1)
    gate_up_first(1)
    gather_far(1, 0)
    gather_y(3, 0)
    gather_z()
    hid_start(0)
    gate_up_pass(0)
    gather_y(1, 1)
    gather_twin(1, 0)
    gate_up_start(1)
    gather_far(3, 0)
    gather_y(2, 0)
    gate_up_cross(0)
    hid_cross(0)
    gather_twin(3, 0)
    gate_up_pass(1)
    gather_far(1, 1)
    hid_start(3)
    gather_far(2, 0)
    hid_pass(0)
    gate_up_start(3)
    gather_twin(1, 1)
    gather_twin(2, 0)
    hid_start(1)
    gate_up_pass(3)
    hid_cross(3)
    gate_up_start(2)
    hid_start(2)
    hid_pass(3)
    hid_cross(1)
    gate_up_pass(2)
    gate_up_cross(3)
    hid_cross(2)
    gate_up_cross(1)
    hid_pass(1)
    pointwise(3)
    gate_up_cross(2)
    hid_pass(2)
    pointwise(1)
    spread_pair(3)
    pointwise(2)
    down_start(2)
    spread_far(3)
    spread_pair(2)
    down_start(1)
    spread_pair(1)
    input_near(3)
    input_rows(3)
    spread_far(2)
    down_far(1)
    input_fold(3)
    down_start(3)
    spread_far(1)
    pointwise(0)
    down_far(2)
    input_near(2)
    input_rows(2)
    input_fold(2)
    spread_pair(0)
    input_pass(3)
    down_far(3)
    down_last(1)
    input_near(1)
    input_rows(1)
    input_pass(2)
    down_start(0)
    weight_pair(2)
    input_fold(1)
    down_last(2)
    input_own(2)
    spread_far(0)
    weight_pair(3)
    weight_down(1)
    input_pass(1)
    down_last(3)
    down_far(0)
    input_near(0)
    input_rows(0)
    down_last(0)
    weight_pair(0)
    input_own(3)
    input_own(1)
    input_far()
    input_fold(0)
    weight_down(3)
    weight_down(2)
    weight_pair(1)
    input_pass(0)
    weight_down(0)
    input_own(0)
    input_out()
    assert arrived == set(groups)
    all_sent()
    for k in range(3):
        moved(3 + k, stage.at[k])
    moved(6, gout)


def hand_over(*refs):
    sems = refs[-1]
    inward, outward = [], []
    for n in (1, 2, 3, 0):
        src, dst, mid = refs[n], refs[4 + n], refs[8 + n]
        rows = src.shape[0]
        parts = HAND_PARTS if n else 1
        for p in range(parts):
            at = pl.ds(p * (rows // parts), rows // parts)
            inward.append(pltpu.make_async_copy(src.at[at], mid.at[at], sems.at[0, n, p]))
            outward.append(pltpu.make_async_copy(mid.at[at], dst.at[at], sems.at[1, n, p]))
    for copy in inward:
        copy.start()
    for arrived, copy in zip(inward, outward):
        arrived.wait()
        copy.start()
    for copy in outward:
        copy.wait()


def local(tokens, w_gate, w_up, w_down, grad_out):
    piece, d = tokens.shape
    ff = w_gate.shape[0]
    ffb, chunk = ff // 8, 8 * piece
    hbm = pl.BlockSpec(memory_space=pl.ANY)

    def vmem(*shape, dtype=BF16):
        return pltpu.VMEM(shape, dtype)

    scratch = [
        vmem(4, 4, 2, 2, piece, d),
        vmem(3, 4, 2, ffb, d),
        vmem(4, 4, 2, 2, ffb, chunk),
        vmem(4, 2, 2, ffb, chunk),
        vmem(4, 2, 2, 2, ffb, chunk),
        vmem(4, 2, ffb, chunk),
        vmem(4, 2, 4, ffb, chunk),
        vmem(4, 4, ffb, chunk),
        vmem(4, ffb, chunk),
        vmem(4, 2, ffb, chunk),
        vmem(4, 4, 2, 2, ffb, chunk),
        vmem(4, 2, 4, ffb, chunk),
        vmem(3, 4, 2, ffb, d, dtype=F32),
        vmem(3, 4, 2, ffb, d),
        vmem(2, 4, chunk, 2 * ffb),
        vmem(4, chunk, d, dtype=F32),
        vmem(4, chunk // 2, d),
        vmem(4, chunk // 2, d),
        vmem(4, 4, piece, d),
        vmem(4, piece, d),
        vmem(4, 2, piece, d),
        vmem(4, piece, d),
        vmem(piece, d),
        vmem(2, piece, d),
        vmem(piece, d),
        pltpu.SemaphoreType.DMA((26,)),
        pltpu.SemaphoreType.DMA((120,)),
        pltpu.SemaphoreType.DMA((8,)),
    ]
    weight = jax.ShapeDtypeStruct((ff, d), BF16)
    held = pl.pallas_call(
        body,
        out_shape=(jax.ShapeDtypeStruct((piece, d), BF16), weight, weight, weight),
        in_specs=[hbm] * 5,
        out_specs=(hbm,) * 4,
        scratch_shapes=scratch,
        compiler_params=pltpu.CompilerParams(
            collective_id=0, has_side_effects=True, vmem_limit_bytes=60 * 2 ** 20
        ),
        cost_estimate=pl.CostEstimate(
            flops=16 * 4 * chunk * ff * d, bytes_accessed=12 * ff * d, transcendentals=4 * chunk * ffb
        ),
    )(tokens, w_gate, w_up, w_down, grad_out)
    return pl.pallas_call(
        hand_over,
        out_shape=tuple(jax.ShapeDtypeStruct(one.shape, one.dtype) for one in held),
        in_specs=[hbm] * 4,
        out_specs=(hbm,) * 4,
        scratch_shapes=[vmem(*one.shape) for one in held] + [pltpu.SemaphoreType.DMA((2, 4, HAND_PARTS))],
        compiler_params=pltpu.CompilerParams(vmem_limit_bytes=60 * 2 ** 20),
        cost_estimate=pl.CostEstimate(flops=0, bytes_accessed=12 * ff * d, transcendentals=0),
    )(*held)


def solution(mesh):
    spec = P("row", "col")
    return jax.shard_map(
        local, mesh=mesh, in_specs=(spec,) * 5, out_specs=(spec,) * 4, check_vma=False
    )
```

```python
import jax
import jax.numpy as jnp
from jax import lax
from jax.experimental import pallas as pl
from jax.experimental.pallas import tpu as pltpu
from jax.sharding import PartitionSpec as P

NY, NZ, NX = 4, 4, 4
F32, BF16 = jnp.float32, jnp.bfloat16
HAND_PARTS = 1


def mm(a, b, dims):
    return lax.dot_general(a, b, (dims, ((), ())), preferred_element_type=F32)


def body(
    tok_hbm, wg_hbm, wu_hbm, wd_hbm, out_hbm,
    gin_hbm, dg_hbm, du_hbm, dd_hbm,
    tg, w, px, rxt, rxf, rz, pz, rzz, rzt, rzf, az, ax, acc, stage, trans,
    part, gs, gc, ys, yt, yf, zs, zq, zr, gout,
    send, recv, local,
):
    row, col = lax.axis_index("row"), lax.axis_index("col")
    y, zh, core = row // 8, (row // 2) % 4, row % 2
    zl, x = col // 4, col % 4

    def at_row(y_, zh_, core_):
        return {"row": (y_ * 4 + zh_) * 2 + core_, "col": col}

    def at_col(zl_, x_):
        return {"row": row, "col": zl_ * 4 + x_}

    y_up, y_dn = at_row((y + 1) % 4, zh, core), at_row((y + 3) % 4, zh, core)
    zh_up, zh_dn = at_row(y, (zh + 1) % 4, core), at_row(y, (zh + 3) % 4, core)
    twin = at_row(y, zh, 1 - core)
    x_up, x_dn = at_col(zl, (x + 1) % 4), at_col(zl, (x + 3) % 4)
    z_pair = at_col(1 - zl, x)
    partners = [y_up, y_dn, zh_up, zh_dn, twin, x_up, x_dn, z_pair]

    sends, groups, arrived = {}, {}, set()
    sent_refs = {
        "xt": rxt, "xf": rxf, "xz": rz, "zz": rzz, "zt": rzt, "zf": rzf,
        "gz": az.at[:, 0, 1], "gx0": az.at[:, 3], "gx1": az.at[:, 1], "gt": az.at[:, 2],
        "hx0": ax.at[:, 0, 3], "hx1": ax.at[:, 0, 1], "ht": ax.at[:, 0, 2], "hz": ax.at[:, 1],
        "cc": gc, "yt": yt, "yf": yf, "zq": zq, "zr": zr,
        "az1": tg.at[3, 0, 0], "az3": tg.at[1, 0, 0], "at": tg.at[2, 0, 0],
        "ay1": tg.at[:, 3, 0], "ay3": tg.at[:, 1, 0], "ax": tg.at[:, 2, 0], "ac": tg.at[:, :, 1],
    }

    def copy_of(src, dst, send_at, recv_at, device):
        return pltpu.make_async_remote_copy(
            src_ref=src, dst_ref=dst, send_sem=send.at[send_at], recv_sem=recv.at[recv_at],
            device_id=device, device_id_type=pl.DeviceIdType.MESH,
        )

    def push(key, src, dst, device, whole=None):
        send_at = sends.setdefault(key[0], len(sends))
        recv_at, _ = groups.setdefault(key, (len(groups), dst if whole is None else whole))
        copy_of(src, dst, send_at, recv_at, device).start()

    def arrive(*keys):
        for key in keys:
            if key not in arrived:
                arrived.add(key)
                recv_at, whole = groups[key]
                copy_of(whole, whole, 0, recv_at, twin).wait_recv()

    def all_sent():
        for kind, send_at in sends.items():
            copy_of(sent_refs[kind], sent_refs[kind], send_at, 0, twin).wait_send()

    def move(n, src, dst):
        copy = pltpu.make_async_copy(src, dst, local.at[n])
        copy.start()
        return copy

    def moved(n, whole):
        pltpu.make_async_copy(whole, whole, local.at[n]).wait()

    d_model = w.shape[-1]
    ffb = w.shape[-2]
    cut = -(-ffb // 32) * 16
    chunk = px.shape[-1]
    halves = (pl.ds(0, cut), pl.ds(cut, ffb - cut))
    n_tile = min(256, d_model)

    def hbm_rows(j, h):
        first = ((x + j) % 4) * (2 * ffb) + (zl if h == 0 else 1 - zl) * ffb
        return pl.ds(pl.multiple_of(first, 16), ffb)

    tok_in = [move(6, tok_hbm, tg.at[0, 0, 0, 0]), move(7, out_hbm, tg.at[0, 0, 0, 1])]
    for k, src in enumerate((wg_hbm, wu_hbm, wd_hbm)):
        for j in range(4):
            for h in range(2):
                move(k, src.at[hbm_rows(j, h)], w.at[k, j, h])

    barrier = pltpu.get_barrier_semaphore()
    for partner in partners:
        pl.semaphore_signal(barrier, inc=1, device_id=partner, device_id_type=pl.DeviceIdType.MESH)
    for copy in tok_in:
        copy.wait()
    pl.semaphore_wait(barrier, len(partners))

    half = chunk // 16
    first, second = pl.ds(0, half), pl.ds(half, half)
    both = pl.ds(0, 2)

    def gather_start():
        for s in (0, 1):
            own = tg.at[0, 0, 0, s]
            push(("ay1", 0, s), own, tg.at[0, 3, 0, s], y_up)
            push(("ay3", 0, s), own, tg.at[0, 1, 0, s], y_dn)
            push(("ac", 0, s, 0), own, tg.at[0, 0, 1, s], twin, tg.at[0, pl.ds(0, 2), 1, s])
            push(("az1", s), own, tg.at[3, 0, 0, s], zh_up)
            push(("az3", s), own, tg.at[1, 0, 0, s], zh_dn)

    def gather_z():
        arrive(("az1", 0), ("az1", 1))
        push(("at",), tg.at[3, 0, 0, :, first], tg.at[2, 0, 0, :, first], zh_up, tg.at[2, 0, 0])
        arrive(("az3", 0), ("az3", 1))
        push(("at",), tg.at[1, 0, 0, :, second], tg.at[2, 0, 0, :, second], zh_dn, tg.at[2, 0, 0])

    def kind(c, s):
        return s if c < 2 else both

    def gather_y(c, s):
        if c == 1:
            arrive(("az3", s))
        elif c == 3:
            arrive(("az1", 0), ("az1", 1))
        else:
            arrive(("at",))
        own = tg.at[c, 0, 0, kind(c, s)]
        push(("ay1", c, s), own, tg.at[c, 3, 0, kind(c, s)], y_up)
        push(("ay3", c, s), own, tg.at[c, 1, 0, kind(c, s)], y_dn)

    def gather_near(c, s):
        far = tg.at[c, 2, 0, kind(c, s)]
        arrive(("ay3", c, s))
        push(("ax", c, s), tg.at[c, 1, 0, kind(c, s), second], tg.at[c, 2, 0, kind(c, s), second], y_dn, far)
        if c == 0:
            push(("ac", 0, s, 0), tg.at[0, 1, 0, s], tg.at[0, 1, 1, s], twin, tg.at[0, pl.ds(0, 2), 1, s])

    def gather_far(c, s):
        far = tg.at[c, 2, 0, kind(c, s)]
        arrive(("ay1", c, s))
        push(("ax", c, s), tg.at[c, 3, 0, kind(c, s), first], tg.at[c, 2, 0, kind(c, s), first], y_up, far)
        if c == 0:
            push(("ac", 0, s, 1), tg.at[0, 3, 0, s], tg.at[0, 3, 1, s], twin, tg.at[0, pl.ds(2, 2), 1, s])
        else:
            gather_near(c, s)

    def gather_twin(c, s):
        arrive(("ax", c, s))
        if c == 0:
            push(("ac", 0, s, 1), tg.at[0, 2, 0, s], tg.at[0, 2, 1, s], twin, tg.at[0, pl.ds(2, 2), 1, s])
        else:
            push(("ac", c, s), tg.at[c, :, 0, kind(c, s)], tg.at[c, :, 1, kind(c, s)], twin)

    def gathered(s, c):
        if c == 0:
            arrive(("ac", 0, s, 0), ("ac", 0, s, 1))
        else:
            arrive(("ac", c, s if c < 2 else 0))

    def rows_of(s, c):
        return tg[c, :, :, s].reshape(chunk, d_model)

    def product(k, s, i, pair):
        part = w[k, 2 * pair:2 * pair + 2].reshape(4 * ffb, d_model)
        out = mm(part, rows_of(s, i), ((1,), (1,)))
        return out.astype(BF16).reshape(2, 2, ffb, chunk)

    def gate_up_first(part_at):
        if part_at == 0:
            moved(0, w.at[0])
            moved(1, w.at[1])
        arrive(("ac", 0, 0, part_at))
        lanes = pl.ds(part_at * (chunk // 2), chunk // 2)
        rows = tg[0, 2 * part_at:2 * part_at + 2, :, 0].reshape(chunk // 2, d_model)
        for pair in (1, 0):
            for k in (0, 1):
                weight = w[k, 2 * pair:2 * pair + 2].reshape(4 * ffb, d_model)
                out = mm(weight, rows, ((1,), (1,))).astype(BF16)
                px[0, 2 * pair:2 * pair + 2, :, k, :, lanes] = out.reshape(2, 2, ffb, chunk // 2)
            if pair == 1:
                push(("xt", 0), px.at[0, 2, 0, :, :, lanes], rxt.at[0, 0, :, :, lanes], x_up, rxt.at[0])
                push(("xt", 0), px.at[0, 2, 1, :, :, lanes], rxt.at[0, 1, :, :, lanes], x_dn, rxt.at[0])
                push(("xf", 0), px.at[0, 3, 0, :, :, lanes], rxf.at[0, 1, 0, :, :, lanes], x_dn, rxf.at[0])
            else:
                push(("xf", 0), px.at[0, 1, 1, :, :, lanes], rxf.at[0, 0, 1, :, :, lanes], x_up, rxf.at[0])

    def gate_up_start(i):
        gathered(0, i)
        for pair in (1, 0):
            for k in (0, 1):
                px[i, 2 * pair:2 * pair + 2, :, k] = product(k, 0, i, pair)
            if pair == 1:
                push(("xt", i), px.at[i, 2, 0], rxt.at[i, 0], x_up, rxt.at[i])
                push(("xt", i), px.at[i, 2, 1], rxt.at[i, 1], x_dn, rxt.at[i])
                push(("xf", i), px.at[i, 3, 0], rxf.at[i, 1, 0], x_dn, rxf.at[i])
            else:
                push(("xf", i), px.at[i, 1, 1], rxf.at[i, 0, 1], x_up, rxf.at[i])

    def gate_up_pass(i):
        arrive(("xt", i))
        px[i, 1, 0] = (px[i, 1, 0].astype(F32) + rxt[i, 0].astype(F32)).astype(BF16)
        push(("xf", i), px.at[i, 1, 0], rxf.at[i, 0, 0], x_up, rxf.at[i])
        px[i, 3, 1] = (px[i, 3, 1].astype(F32) + rxt[i, 1].astype(F32)).astype(BF16)
        push(("xf", i), px.at[i, 3, 1], rxf.at[i, 1, 1], x_dn, rxf.at[i])

    def gate_up_sum(i, h):
        return px[i, 0, h].astype(F32) + rxf[i, 0, h].astype(F32) + rxf[i, 1, h].astype(F32)

    def gate_up_cross(i):
        arrive(("xf", i))
        px[i, 0, 1] = gate_up_sum(i, 1).astype(BF16)
        push(("xz", i), px.at[i, 0, 1], rz.at[i], z_pair)

    def hid_start(i):
        if i == 0:
            moved(2, w.at[2])
        gathered(1, i)
        for pair in (1, 0):
            out = product(2, 1, i, pair)
            for j in range(2):
                for h in range(2):
                    pz[i, h, 2 * pair + j] = out[j, h]
        push(("zz", i), pz.at[i, 1], rzz.at[i], z_pair)

    def hid_cross(i):
        arrive(("zz", i))
        pz[i, 0] = (pz[i, 0].astype(F32) + rzz[i].astype(F32)).astype(BF16)
        for ab, (to, back, far, near) in enumerate(((x_up, x_dn, 0, 3), (x_dn, x_up, 1, 1))):
            push(("zt", i), pz.at[i, 0, 2, halves[ab]], rzt.at[i, halves[ab]], to, rzt.at[i])
        push(("zf", i), pz.at[i, 0, 3, halves[0]], rzf.at[i, 1, halves[0]], x_dn, rzf.at[i])
        push(("zf", i), pz.at[i, 0, 1, halves[1]], rzf.at[i, 0, halves[1]], x_up, rzf.at[i])

    def hid_pass(i):
        arrive(("zt", i))
        for ab, (j, to) in enumerate(((1, x_up), (3, x_dn))):
            part = pz[i, 0, j, halves[ab]].astype(F32) + rzt[i, halves[ab]].astype(F32)
            pz[i, 0, j, halves[ab]] = part.astype(BF16)
            push(("zf", i), pz.at[i, 0, j, halves[ab]], rzf.at[i, ab, halves[ab]], to, rzf.at[i])

    def pointwise(i):
        arrive(("xz", i))
        pre = gate_up_sum(i, 0) + rz[i].astype(F32)
        gate_pre, up_pre = pre[0], pre[1]
        arrive(("zf", i))
        hid_grad = pz[i, 0, 0].astype(F32) + rzf[i, 0].astype(F32) + rzf[i, 1].astype(F32)
        logistic = 1.0 / (1.0 + jnp.exp(-gate_pre))
        activated = gate_pre * logistic
        az[i, 0, 0, 0] = (hid_grad * up_pre * logistic * (1.0 + gate_pre * (1.0 - logistic))).astype(BF16)
        az[i, 0, 0, 1] = (hid_grad * activated).astype(BF16)
        push(("gz", i), az.at[i, 0, 0], az.at[i, 0, 1], z_pair)
        push(("gx0", i, 0), az.at[i, 0, 0], az.at[i, 3, 0], x_up)
        push(("gx1", i, 0), az.at[i, 0, 0], az.at[i, 1, 0], x_dn)
        ax[i, 0, 0] = (activated * up_pre).astype(BF16)

    def spread_pair(i):
        arrive(("gz", i))
        push(("gx0", i, 1), az.at[i, 0, 1], az.at[i, 3, 1], x_up)
        push(("gx1", i, 1), az.at[i, 0, 1], az.at[i, 1, 1], x_dn)

    def spread_far(i):
        arrive(("gx0", i, 0))
        push(("gt", i), az.at[i, 3, 0], az.at[i, 2, 0], x_up, az.at[i, 2])
        arrive(("gx1", i, 1))
        push(("gt", i), az.at[i, 1, 1], az.at[i, 2, 1], x_dn, az.at[i, 2])

    def down_start(i):
        push(("hx0", i), ax.at[i, 0, 0], ax.at[i, 0, 3], x_up)
        push(("hx1", i), ax.at[i, 0, 0], ax.at[i, 0, 1], x_dn)
        push(("hz", i), ax.at[i, 0, 0], ax.at[i, 1, 0], z_pair, ax.at[i, 1])

    def down_far(i):
        arrive(("hx0", i))
        push(("ht", i), ax.at[i, 0, 3, halves[0]], ax.at[i, 0, 2, halves[0]], x_up, ax.at[i, 0, 2])
        push(("hz", i), ax.at[i, 0, 3], ax.at[i, 1, 3], z_pair, ax.at[i, 1])
        arrive(("hx1", i))
        push(("ht", i), ax.at[i, 0, 1, halves[1]], ax.at[i, 0, 2, halves[1]], x_dn, ax.at[i, 0, 2])
        push(("hz", i), ax.at[i, 0, 1], ax.at[i, 1, 1], z_pair, ax.at[i, 1])

    def down_last(i):
        arrive(("ht", i))
        push(("hz", i), ax.at[i, 0, 2], ax.at[i, 1, 2], z_pair, ax.at[i, 1])

    def input_near(i):
        arrive(("gz", i), ("gx0", i, 0), ("gx1", i, 1), ("gx1", i, 0), ("gx0", i, 1))
        for j in (0, 1, 3):
            for k in (0, 1):
                trans[k, j] = az[i, j, :, k].reshape(2 * ffb, chunk).T
        for n in range(d_model // n_tile):
            cols = pl.ds(n * n_tile, n_tile)
            part[i, :, cols] = sum(
                mm(trans[k, j], w[k, j, :, :, cols].reshape(2 * ffb, n_tile), ((1,), (0,)))
                for k in (0, 1) for j in (0, 1, 3)
            )

    def input_rows(i):
        arrive(("gt", i))
        for k in (0, 1):
            trans[k, 2] = az[i, 2, :, k].reshape(2 * ffb, chunk).T
        for n in range(d_model // n_tile):
            cols = pl.ds(n * n_tile, n_tile)
            out = part[i, :, cols] + sum(
                mm(trans[k, 2], w[k, 2, :, :, cols].reshape(2 * ffb, n_tile), ((1,), (0,)))
                for k in (0, 1)
            )
            part[i, :, cols] = out
            other = out.reshape(4, 2, piece, n_tile)[:, 1].reshape(chunk // 2, n_tile)
            gs[i, :, cols] = other.astype(BF16)
        push(("cc", i), gs.at[i], gc.at[i], twin)

    piece = chunk // 8

    def at_y(yr):
        return pl.ds(yr * 2 * piece, piece)

    def at_other(yr):
        return pl.ds(yr * piece, piece)

    def input_fold(i):
        arrive(("cc", i))
        part[i, at_y(0)] = part[i, at_y(0)] + gc[i, at_other(0)].astype(F32)
        for yr in (2, 1, 3):
            ys[i, yr] = (part[i, at_y(yr)] + gc[i, at_other(yr)].astype(F32)).astype(BF16)
            if yr == 2:
                push(("yt", i), ys.at[i, 2, first], yt.at[i, first], y_up, yt.at[i])
                push(("yt", i), ys.at[i, 2, second], yt.at[i, second], y_dn, yt.at[i])
            elif yr == 1:
                push(("yf", i), ys.at[i, 1, second], yf.at[i, 0, second], y_up, yf.at[i])
            else:
                push(("yf", i), ys.at[i, 3, first], yf.at[i, 1, first], y_dn, yf.at[i])

    def input_pass(i):
        arrive(("yt", i))
        for ab, (yr, rows, to) in enumerate(((1, first, y_up), (3, second, y_dn))):
            ys[i, yr, rows] = (ys[i, yr, rows].astype(F32) + yt[i, rows].astype(F32)).astype(BF16)
            push(("yf", i), ys.at[i, yr, rows], yf.at[i, ab, rows], to, yf.at[i])

    def input_own(i):
        arrive(("yf", i))
        part[i, at_y(0)] = part[i, at_y(0)] + yf[i, 0].astype(F32) + yf[i, 1].astype(F32)
        if i == 1:
            zs[1, second] = part[1, pl.ds(half, half)].astype(BF16)
            push(("zr",), zs.at[1, second], zr.at[0, second], zh_up, zr)
        elif i == 2:
            zs[2] = part[2, at_y(0)].astype(BF16)
            push(("zq",), zs.at[2, first], zq.at[first], zh_up, zq)
            push(("zq",), zs.at[2, second], zq.at[second], zh_dn, zq)
        elif i == 3:
            arrive(("zq",))
            zs[3, first] = part[3, pl.ds(0, half)].astype(BF16)
            zs[3, second] = (part[3, pl.ds(half, half)] + zq[second].astype(F32)).astype(BF16)
            push(("zr",), zs.at[3], zr.at[1], zh_dn, zr)

    def input_far():
        arrive(("zq",))
        zs[1, first] = (part[1, pl.ds(0, half)] + zq[first].astype(F32)).astype(BF16)
        push(("zr",), zs.at[1, first], zr.at[0, first], zh_up, zr)

    def input_out():
        arrive(("zr",))
        gout[...] = (
            part[0, at_y(0)] + zr[0].astype(F32) + zr[1].astype(F32)
        ).astype(BF16)
        move(6, gout, gin_hbm)

    scale = float(NY * chunk) ** -0.5

    added = [0, 0, 0]

    def weight_rows(k, i):
        added[k] += 1
        s = 0 if k < 2 else 1
        for pair in (0, 1):
            js = slice(2 * pair, 2 * pair + 2)
            if k < 2:
                left = az[i, js, :, k].reshape(4 * ffb, chunk)
            else:
                left = jnp.concatenate(
                    [ax[i, h, j] for j in (2 * pair, 2 * pair + 1) for h in (0, 1)], axis=0
                )
            for n in range(d_model // n_tile):
                cols = pl.ds(n * n_tile, n_tile)
                right = tg[i, :, :, s, :, cols].reshape(chunk, n_tile)
                out = mm(left, right, ((1,), (0,))).reshape(2, 2, ffb, n_tile)
                if added[k] > 1:
                    out = out + acc[k, js, :, :, cols]
                if added[k] < NY:
                    acc[k, js, :, :, cols] = out
                else:
                    stage[k, js, :, :, cols] = (out * scale).astype(BF16)
            if added[k] == NY:
                out_hbm_k = (dg_hbm, du_hbm, dd_hbm)[k]
                for j in (2 * pair, 2 * pair + 1):
                    for h in range(2):
                        move(3 + k, stage.at[k, j, h], out_hbm_k.at[hbm_rows(j, h)])

    def weight_pair(i):
        weight_rows(0, i)
        weight_rows(1, i)

    def weight_down(i):
        arrive(("hz", i))
        weight_rows(2, i)

    gather_start()
    gather_near(0, 0)
    gather_far(0, 0)
    gather_far(0, 1)
    gather_near(0, 1)
    gate_up_first(0)
    gather_y(1, 0)
    gather_twin(0, 0)
    gate_up_first(1)
    gather_z()
    gather_twin(0, 1)
    gather_far(1, 0)
    gather_y(1, 1)
    hid_start(0)
    gather_y(3, 0)
    gate_up_pass(0)
    gather_twin(1, 0)
    gather_far(1, 1)
    gate_up_start(1)
    gather_far(3, 0)
    gather_twin(1, 1)
    gather_y(2, 0)
    hid_cross(0)
    hid_start(1)
    gather_twin(3, 0)
    gate_up_pass(1)
    gather_far(2, 0)
    hid_pass(0)
    gate_up_start(3)
    hid_start(3)
    gate_up_cross(1)
    gather_twin(2, 0)
    hid_cross(1)
    gate_up_start(2)
    hid_start(2)
    gate_up_pass(3)
    hid_pass(1)
    gate_up_cross(0)
    gate_up_pass(2)
    hid_cross(3)
    hid_cross(2)
    pointwise(1)
    hid_pass(2)
    gate_up_cross(2)
    spread_pair(1)
    gate_up_cross(3)
    hid_pass(3)
    down_start(1)
    pointwise(2)
    spread_far(1)
    down_far(1)
    input_near(1)
    pointwise(3)
    input_rows(1)
    spread_pair(2)
    down_last(1)
    weight_pair(1)
    input_fold(1)
    spread_pair(3)
    spread_far(2)
    input_pass(1)
    down_start(3)
    input_near(2)
    spread_far(3)
    pointwise(0)
    input_near(3)
    input_rows(2)
    down_start(2)
    spread_pair(0)
    input_fold(2)
    down_far(3)
    down_start(0)
    input_rows(3)
    input_own(1)
    input_pass(2)
    weight_pair(2)
    input_fold(3)
    weight_down(1)
    down_far(2)
    spread_far(0)
    input_own(2)
    input_near(0)
    down_last(2)
    down_last(3)
    input_pass(3)
    down_far(0)
    weight_pair(3)
    input_rows(0)
    down_last(0)
    input_own(3)
    input_fold(0)
    input_far()
    weight_down(3)
    weight_pair(0)
    input_pass(0)
    weight_down(0)
    weight_down(2)
    input_own(0)
    input_out()
    assert arrived == set(groups)
    all_sent()
    for k in range(3):
        moved(3 + k, stage.at[k])
    moved(6, gout)


def hand_over(*refs):
    sems = refs[-1]
    inward, outward = [], []
    for n in (1, 2, 3, 0):
        src, dst, mid = refs[n], refs[4 + n], refs[8 + n]
        rows = src.shape[0]
        parts = HAND_PARTS if n else 1
        for p in range(parts):
            at = pl.ds(p * (rows // parts), rows // parts)
            inward.append(pltpu.make_async_copy(src.at[at], mid.at[at], sems.at[0, n, p]))
            outward.append(pltpu.make_async_copy(mid.at[at], dst.at[at], sems.at[1, n, p]))
    for copy in inward:
        copy.start()
    for arrived, copy in zip(inward, outward):
        arrived.wait()
        copy.start()
    for copy in outward:
        copy.wait()


def local(tokens, w_gate, w_up, w_down, grad_out):
    piece, d = tokens.shape
    ff = w_gate.shape[0]
    ffb, chunk = ff // 8, 8 * piece
    hbm = pl.BlockSpec(memory_space=pl.ANY)

    def vmem(*shape, dtype=BF16):
        return pltpu.VMEM(shape, dtype)

    scratch = [
        vmem(4, 4, 2, 2, piece, d),
        vmem(3, 4, 2, ffb, d),
        vmem(4, 4, 2, 2, ffb, chunk),
        vmem(4, 2, 2, ffb, chunk),
        vmem(4, 2, 2, 2, ffb, chunk),
        vmem(4, 2, ffb, chunk),
        vmem(4, 2, 4, ffb, chunk),
        vmem(4, 4, ffb, chunk),
        vmem(4, ffb, chunk),
        vmem(4, 2, ffb, chunk),
        vmem(4, 4, 2, 2, ffb, chunk),
        vmem(4, 2, 4, ffb, chunk),
        vmem(3, 4, 2, ffb, d, dtype=F32),
        vmem(3, 4, 2, ffb, d),
        vmem(2, 4, chunk, 2 * ffb),
        vmem(4, chunk, d, dtype=F32),
        vmem(4, chunk // 2, d),
        vmem(4, chunk // 2, d),
        vmem(4, 4, piece, d),
        vmem(4, piece, d),
        vmem(4, 2, piece, d),
        vmem(4, piece, d),
        vmem(piece, d),
        vmem(2, piece, d),
        vmem(piece, d),
        pltpu.SemaphoreType.DMA((26,)),
        pltpu.SemaphoreType.DMA((120,)),
        pltpu.SemaphoreType.DMA((8,)),
    ]
    weight = jax.ShapeDtypeStruct((ff, d), BF16)
    held = pl.pallas_call(
        body,
        out_shape=(jax.ShapeDtypeStruct((piece, d), BF16), weight, weight, weight),
        in_specs=[hbm] * 5,
        out_specs=(hbm,) * 4,
        scratch_shapes=scratch,
        compiler_params=pltpu.CompilerParams(
            collective_id=0, has_side_effects=True, vmem_limit_bytes=60 * 2 ** 20
        ),
        cost_estimate=pl.CostEstimate(
            flops=16 * 4 * chunk * ff * d, bytes_accessed=12 * ff * d, transcendentals=4 * chunk * ffb
        ),
    )(tokens, w_gate, w_up, w_down, grad_out)
    return pl.pallas_call(
        hand_over,
        out_shape=tuple(jax.ShapeDtypeStruct(one.shape, one.dtype) for one in held),
        in_specs=[hbm] * 4,
        out_specs=(hbm,) * 4,
        scratch_shapes=[vmem(*one.shape) for one in held] + [pltpu.SemaphoreType.DMA((2, 4, HAND_PARTS))],
        compiler_params=pltpu.CompilerParams(vmem_limit_bytes=60 * 2 ** 20),
        cost_estimate=pl.CostEstimate(flops=0, bytes_accessed=12 * ff * d, transcendentals=0),
    )(*held)


def solution(mesh):
    spec = P("row", "col")
    return jax.shard_map(
        local, mesh=mesh, in_specs=(spec,) * 5, out_specs=(spec,) * 4, check_vma=False
    )
```
